256 devices in a mesh: week: 32 (over z, y), region: 8 (over x, core).
Axes of the slice: x: 4, y: 4, z: 8, core: 2. Of those that a mesh axis runs over, the one named last changes fastest.
Arguments:
- stock_start: float32 [128, 8, 32768], P('week', 'region'), may hold values from 0 to 2
- ship_start: float32 [128, 8, 32768], P('week', 'region'), may hold values from 0 to 1
- dual_start: float32 [128, 8, 32768], P('week', 'region'), may hold values from -12 to 12
- demand: float32 [128, 8, 32768], P('week', 'region'), may hold values from 0.2 to 6
- cost_hold: float32 [128, 8, 32768], P('week', 'region'), may hold values from 0.2 to 6
- cost_ship: float32 [128, 8, 32768], P('week', 'region'), may hold values from 0.2 to 6
- ship_cap: int32 [128, 8, 32768], P('week', 'region'), may hold values from 1 to 3
- lead_weeks: int32 [8, 32768], P('region'), may hold values from 1 to 2
- lane_mix: float32 [8, 128, 128], P('region'), may hold values from 0 to 1, as said below
Outputs:
- stock_final: float32 [128, 8, 32768], P('week', 'region')
- ship_final: float32 [128, 8, 32768], P('week', 'region')
- dual_final: float32 [128, 8, 32768], P('week', 'region')
- projected: float32 [128, 8, 32768], P('week', 'region')
The draws below stay inside these ranges and needn't reach their ends.
Inputs may be any that keep to these rules, and one draw needn't show every extreme that they name: `lane_mix`: nonnegative shares.
All inputs are finite; a program needn't handle non-finite values.
Results may differ from the reference program's by a relative error of at most 0.0001.
Values sent between devices are 32-bit elements; how exact they have to be, the bound alone decides.
A program may use at most 64 MiB of HBM per device.

```python
import math
import jax
import jax.numpy as jnp
from jax import lax

LEAD_MAX = 2
PANEL = 128
ITERS = 2
ITEM_DEV = 32768
WEEKS = 128
GROUPS = 8


def season_ramp():
    week_index = jnp.arange(WEEKS).astype(jnp.float32)
    ramp = 1.0 + 2.0 * week_index / (WEEKS - 1)
    return jnp.broadcast_to(ramp[:, None, None], (WEEKS, GROUPS, ITEM_DEV))


def positive_season(key):
    ramp = season_ramp()
    shape = (WEEKS, GROUPS, ITEM_DEV)
    noise = jax.random.uniform(key, shape, jnp.float32, math.log(0.2), math.log(2.0))
    return (ramp * jnp.exp(noise)).astype(jnp.float32)


def draw_demand(key, part):
    return positive_season(jax.random.fold_in(key, 11))


def draw_cost_hold(key, part):
    return positive_season(jax.random.fold_in(key, 23))


def draw_cost_ship(key, part):
    return positive_season(jax.random.fold_in(key, 37))


def draw_dual_start(key, part):
    inner = jax.random.fold_in(key, 41)
    ramp = season_ramp()
    shape = (WEEKS, GROUPS, ITEM_DEV)
    noise = jnp.clip(jax.random.normal(inner, shape, jnp.float32), -4.0, 4.0)
    return (noise * ramp).astype(jnp.float32)


def draw_lane_mix(key, part):
    first = jax.random.fold_in(key, 53)
    second = jax.random.fold_in(key, 59)
    identity = jnp.eye(PANEL, dtype=jnp.float32)
    diagonal = jax.random.uniform(first, (GROUPS, PANEL), jnp.float32, 0.5, 0.8)
    spread = jax.random.uniform(second, (GROUPS, PANEL, PANEL), jnp.float32, 0.0, 0.5 / PANEL)
    return (spread * (1.0 - identity) + diagonal[:, :, None] * identity).astype(jnp.float32)


def place_ends(entries, own_key, smallest, high):
    longest = entries.shape.index(max(entries.shape))
    spots = []
    for shift in (0, 1):
        where = [jax.random.randint(jax.random.fold_in(own_key, axis), (), 0, length) for axis, length in enumerate(entries.shape)]
        where[longest] = (where[longest] + shift) % entries.shape[longest]
        spots.append(tuple(where))
    return entries.at[spots[0]].set(smallest).at[spots[1]].set(high)


def levels(own_key, dims, pieces, least, largest):
    level, own = 1.0, jax.random.fold_in(own_key, 6)
    for position, parts in pieces:
        heights = jnp.exp(jax.random.uniform(jax.random.fold_in(own, position), (parts,), jnp.float32, least / len(pieces), largest / len(pieces)))
        level = level * jnp.repeat(heights, dims[position] // parts).reshape([-1 if axis == position else 1 for axis in range(len(dims))])
    return level


def setup_inputs(seed: int = 0) -> dict:
    seeds = jax.random.split(jax.random.key(seed), 10)
    stock_start = jnp.clip(2.0 * jax.random.uniform(seeds[0], (WEEKS, GROUPS, ITEM_DEV), jnp.float32) ** levels(seeds[0], (WEEKS, GROUPS, ITEM_DEV), ((0, 32), (1, 8)), -0.2, 0.2), 0.0, 2.0)
    ship_start = jnp.clip(1.0 * jax.random.uniform(seeds[1], (WEEKS, GROUPS, ITEM_DEV), jnp.float32) ** levels(seeds[1], (WEEKS, GROUPS, ITEM_DEV), ((0, 32), (1, 8)), -0.2, 0.2), 0.0, 1.0)
    dual_start = draw_dual_start(jax.random.fold_in(seeds[9], 71), 0)
    demand = draw_demand(jax.random.fold_in(seeds[9], 71), 0)
    cost_hold = draw_cost_hold(jax.random.fold_in(seeds[9], 71), 0)
    cost_ship = draw_cost_ship(jax.random.fold_in(seeds[9], 71), 0)
    ship_cap = place_ends(jax.random.randint(seeds[6], (WEEKS, GROUPS, ITEM_DEV), 1, 4), jax.random.fold_in(seeds[6], 1), 1, 3).astype(jnp.int32)
    lead_weeks = place_ends(jax.random.randint(seeds[7], (GROUPS, ITEM_DEV), 1, LEAD_MAX + 1), jax.random.fold_in(seeds[7], 1), 1, LEAD_MAX).astype(jnp.int32)
    lane_mix = draw_lane_mix(jax.random.fold_in(seeds[9], 71), 0)
    return {"stock_start": stock_start, "ship_start": ship_start, "dual_start": dual_start, "demand": demand, "cost_hold": cost_hold, "cost_ship": cost_ship, "ship_cap": ship_cap, "lead_weeks": lead_weeks, "lane_mix": lane_mix}


step_eta = 0.25
eps_move = 1e-06

def from_before(values_in, amount):
    return jnp.concatenate([jnp.zeros_like(values_in[:amount]), values_in[:-amount]], axis=0)

def from_after(values_in, amount):
    return jnp.concatenate([values_in[amount:], jnp.zeros_like(values_in[:amount])], axis=0)

def panel_mix(values_in, lane_mix, transpose):
    panels_view = values_in.reshape(values_in.shape[0], values_in.shape[1], -1, PANEL)
    if transpose:
        mixed = jnp.einsum('wgbj,gkj->wgbk', panels_view, lane_mix, precision=lax.Precision.HIGHEST)
    else:
        mixed = jnp.einsum('wgbk,gkj->wgbj', panels_view, lane_mix, precision=lax.Precision.HIGHEST)
    return mixed.reshape(values_in.shape)

def forward(stock_level, ship_flow, lead_weeks, lane_mix):
    lagged = jnp.zeros_like(ship_flow)
    for offset in range(1, LEAD_MAX + 1):
        lagged = lagged + jnp.where(lead_weeks[None] == offset, from_before(ship_flow, offset), 0.0)
    receipts = jnp.roll(panel_mix(lagged, lane_mix, False), 1, axis=1)
    balance = stock_level - from_before(stock_level, 1) + ship_flow - receipts
    return (balance, receipts)

def adjoint(dual_price, lead_weeks, lane_mix):
    pulled = panel_mix(jnp.roll(dual_price, -1, axis=1), lane_mix, True)
    picked = jnp.zeros_like(dual_price)
    for offset in range(1, LEAD_MAX + 1):
        picked = picked + jnp.where(lead_weeks[None] == offset, from_after(pulled, offset), 0.0)
    return (dual_price - from_after(dual_price, 1), dual_price - picked)

def reference(stock_start, ship_start, dual_start, demand, cost_hold, cost_ship, ship_cap, lead_weeks, lane_mix):
    cap_float = ship_cap.astype(jnp.float32)
    stock_level, ship_flow, dual_price = (stock_start, ship_start, dual_start)
    balance, receipts = forward(stock_level, ship_flow, lead_weeks, lane_mix)
    grad_hold, grad_ship = adjoint(dual_price, lead_weeks, lane_mix)
    primal_step = step_eta
    dual_step = step_eta
    for round_index in range(ITERS):
        new_stock = jnp.maximum(stock_level - primal_step * (cost_hold - grad_hold), 0.0)
        new_ship = jnp.clip(ship_flow - primal_step * (cost_ship - grad_ship), 0.0, cap_float)
        new_balance, receipts = forward(new_stock, new_ship, lead_weeks, lane_mix)
        new_dual = dual_price + dual_step * (demand - 2.0 * new_balance + balance)
        if round_index == 0:
            moved_primal = jnp.sum((new_stock - stock_level) ** 2) + jnp.sum((new_ship - ship_flow) ** 2)
            moved_dual = jnp.sum((new_dual - dual_price) ** 2)
            weight = jnp.sqrt(jnp.sqrt((moved_dual + eps_move) / (moved_primal + eps_move)))
            primal_step = step_eta / weight
            dual_step = step_eta * weight
        if round_index + 1 < ITERS:
            grad_hold, grad_ship = adjoint(new_dual, lead_weeks, lane_mix)
        stock_level, ship_flow, dual_price, balance = (new_stock, new_ship, new_dual, new_balance)
    net_flow = receipts - ship_flow - demand
    projected = jnp.cumsum(net_flow, axis=0)
    return (stock_level, ship_flow, dual_price, projected)
```

```python
import functools

import jax
import jax.numpy as jnp
from jax import lax
from jax.experimental import pallas as pl
from jax.experimental.pallas import tpu as pltpu
from jax.sharding import PartitionSpec as P

PANEL = 128
ROWS = 4
CHUNKS = 4
LAG = 2
STEP_ETA = 0.25
EPS_MOVE = 1e-06
MESH = pl.DeviceIdType.MESH
F32 = jnp.float32
BF16 = jnp.bfloat16


def ring_distance(d, n):
    return min(d % n, -d % n)


def week_offsets(weeks):
    def hops(d):
        return ring_distance(d // 4, max(weeks // 4, 1)) + ring_distance(d % 4, 4)

    return sorted(range(1, weeks), key=lambda d: (-hops(d), d))


def kernel(weeks, regions, panels, *refs):
    (
        stock_in, ship_in, dual_in, demand_in, hold_in, cost_in, cap_in, lead_in, mix_in,
        stock_out, ship_out, dual_out, proj_out,
        v0, s0, y0, dem, ch, cs, cap, lead, mixw,
        w_fwd, w_adj,
        v1, s1, y1, v2, s2, y2, bal1, pj,
        yb0, yo0, yb1, yo1,
        fs_t, fv_t, fb_t, fh_t,
        fs_1, fb_1, fh_1,
        fs_2, fb_2, fh_2,
        m_send, m_recv, s_sum, net, a1, a2, pref,
        row1, rows1, row2, rows2,
        load_sem, out_sem,
        y0_ss, y0_rs, y1_ss, y1_rs, ft_ss, ft_rs, f1_ss, f1_rs, f2_ss, f2_rs,
        m_ss, m_rs, r1_ss, r1_rs, r2_ss, r2_rs, p1_ss, p1_rs, p2_ss, p2_rs,
    ) = refs
    w = lax.axis_index("week")
    r = lax.axis_index("region")
    first = w == 0
    last = w == weeks - 1
    size = panels // CHUNKS
    piece = panels // weeks

    def there(dw, dr):
        return (lax.rem(w + dw + weeks, weeks), lax.rem(r + dr + regions, regions))

    loads = []
    for k, (src, dst) in enumerate(
        (
            (dual_in, y0), (mix_in, mixw), (lead_in, lead), (stock_in, v0), (ship_in, s0),
            (hold_in, ch), (cost_in, cs), (cap_in, cap), (demand_in, dem),
        )
    ):
        cp = pltpu.make_async_copy(src, dst, load_sem.at[k])
        cp.start()
        loads.append(cp)

    w_off = week_offsets(weeks)
    near = [(0, 1), (1, 1), (1, 0), (0, -1), (-1, -1), (-1, 0)]
    far = [(d, 0) for d in w_off] + [(0, d) for d in range(1, regions)]
    partners = list(dict.fromkeys((a % weeks, b % regions) for a, b in near + far))
    barrier = pltpu.get_barrier_semaphore()
    for dw, dr in partners:
        pl.semaphore_signal(barrier, inc=1, device_id=there(dw, dr), device_id_type=MESH)
    pl.semaphore_wait(barrier, len(partners))

    sends = []

    def send(src, dst, ss, rs, to):
        cp = pltpu.make_async_remote_copy(
            src_ref=src, dst_ref=dst, send_sem=ss, recv_sem=rs, device_id=to, device_id_type=MESH
        )
        cp.start()
        sends.append(cp)
        return cp

    def span(c):
        return pl.ds(c * size, size)

    def send_prices(y, yb, yo, ss, rs, c):
        k = 3 * c
        return [
            send(y.at[0:2, span(c)], yb.at[3:5, span(c)], ss.at[k], rs.at[k], there(-1, -1)),
            send(y.at[0:1, span(c)], yo.at[:, span(c)], ss.at[k + 1], rs.at[k + 1], there(-1, 0)),
            send(y.at[1:4, span(c)], yb.at[0:3, span(c)], ss.at[k + 2], rs.at[k + 2], there(0, -1)),
        ]

    def send_arrivals(fs, fv, fb, fh, ss, rs, c):
        k = 3 * c
        return [
            send(fs.at[3:5, span(c)], fb.at[3:5, span(c)], ss.at[k], rs.at[k], there(1, 1)),
            send(fv, fh.at[:, span(c)], ss.at[k + 1], rs.at[k + 1], there(1, 0)),
            send(fs.at[0:3, span(c)], fb.at[0:3, span(c)], ss.at[k + 2], rs.at[k + 2], there(0, 1)),
        ]

    def mix(values, weight):
        hi = values.astype(BF16)
        lo = (values - hi.astype(F32)).astype(BF16)
        both = jnp.dot(jnp.concatenate([hi, lo], axis=1), weight[...], preferred_element_type=F32)
        return both[:, :PANEL] + both[:, PANEL:]

    def pulled_gradients(y, yb, yo, c):
        pulled = mix(yb[:, span(c), :].reshape(5 * size, PANEL), w_adj).reshape(5, size, PANEL)
        pulled = [pulled[k] for k in range(5)]
        pulled[3] = jnp.where(last, 0.0, pulled[3])
        pulled[4] = jnp.where(last, 0.0, pulled[4])
        short = lead[span(c), :] == 1
        rows = [y[t, span(c), :] for t in range(ROWS)]
        after = rows[1:] + [jnp.where(last, 0.0, yo[0, span(c), :])]
        grad_v = [rows[t] - after[t] for t in range(ROWS)]
        grad_s = [rows[t] - jnp.where(short, pulled[t], pulled[t + 1]) for t in range(ROWS)]
        return grad_v, grad_s

    def mix_arrivals(rows, fs, c):
        short = lead[span(c), :] == 1
        lagged = jnp.concatenate(
            [
                jnp.where(short, rows[0], 0.0),
                jnp.where(short, rows[1], rows[0]),
                jnp.where(short, rows[2], rows[1]),
                jnp.where(short, rows[3], rows[2]),
                jnp.where(short, 0.0, rows[3]),
            ],
            axis=0,
        )
        fs[:, span(c), :] = mix(lagged, w_fwd).reshape(5, size, PANEL)

    def arrivals(fb, c):
        early = [jnp.where(first, 0.0, fb[3 + k, span(c), :]) for k in range(2)]
        own = [fb[k, span(c), :] for k in range(3)]
        return early, [early[0], own[0] + early[1], own[1], own[2]]

    def balance_of(v_rows, s_rows, fh, receipts, c):
        before = [jnp.where(first, 0.0, fh[0, span(c), :])] + v_rows[:-1]
        return [v_rows[t] - before[t] + s_rows[t] - receipts[t] for t in range(ROWS)]

    def fold(values):
        return jnp.sum(values.reshape(size // 8, 8, PANEL), axis=0)

    loads[0].wait()
    y0_cp = [send_prices(y0, yb0, yo0, y0_ss, y0_rs, c) for c in range(CHUNKS)]
    loads[1].wait()
    for weight, dest in ((mixw[...], w_fwd), (mixw[...].T, w_adj)):
        hi = weight.astype(BF16)
        lo = (weight - hi.astype(F32)).astype(BF16)
        half = jnp.concatenate([hi, lo], axis=1)
        dest[...] = jnp.concatenate([half, half], axis=0)
    for cp in loads[2:]:
        cp.wait()

    primal = jnp.zeros((8, PANEL), F32)
    dual = jnp.zeros((8, PANEL), F32)
    ft_cp = {}
    y1_cp = {}

    def first_primal(c, primal):
        for cp in y0_cp[c]:
            cp.wait_recv()
        grad_v, grad_s = pulled_gradients(y0, yb0, yo0, c)
        ahead = []
        for t in range(ROWS):
            old_v = v0[t, span(c), :]
            new_v = jnp.maximum(old_v - STEP_ETA * (ch[t, span(c), :] - grad_v[t]), 0.0)
            v1[t, span(c), :] = new_v
            if t == ROWS - 1:
                fv_t[0, span(c), :] = 2.0 * new_v - old_v
            old_s = s0[t, span(c), :]
            top = cap[t, span(c), :].astype(F32)
            new_s = jnp.minimum(
                jnp.maximum(old_s - STEP_ETA * (cs[t, span(c), :] - grad_s[t]), 0.0), top
            )
            s1[t, span(c), :] = new_s
            primal = primal + fold((new_v - old_v) ** 2) + fold((new_s - old_s) ** 2)
            ahead.append(2.0 * new_s - old_s)
        mix_arrivals(ahead, fs_t, c)
        ft_cp[c] = send_arrivals(fs_t, fv_t.at[:, span(c)], fb_t, fh_t, ft_ss, ft_rs, c)
        return primal

    def first_dual(c, dual):
        for cp in ft_cp[c]:
            cp.wait_recv()
        _, receipts = arrivals(fb_t, c)
        v_rows = [2.0 * v1[t, span(c), :] - v0[t, span(c), :] for t in range(ROWS)]
        s_rows = [2.0 * s1[t, span(c), :] - s0[t, span(c), :] for t in range(ROWS)]
        ahead = balance_of(v_rows, s_rows, fh_t, receipts, c)
        for t in range(ROWS):
            moved = STEP_ETA * (dem[t, span(c), :] - ahead[t])
            new_y = y0[t, span(c), :] + moved
            y1[t, span(c), :] = new_y
            dual = dual + fold((new_y - y0[t, span(c), :]) ** 2)
        if c < CHUNKS - 1:
            y1_cp[c] = send_prices(y1, yb1, yo1, y1_ss, y1_rs, c)
        return dual

    for c in range(CHUNKS + LAG):
        if c < CHUNKS:
            primal = first_primal(c, primal)
        if c >= LAG:
            dual = first_dual(c - LAG, dual)

    lane = lax.broadcasted_iota(jnp.int32, (1, PANEL), 1)
    primal = jnp.sum(primal, axis=0, keepdims=True)
    dual = jnp.sum(dual, axis=0, keepdims=True)
    half = PANEL // 2
    mine = jnp.where(
        lane < half, primal + pltpu.roll(primal, half, 1), dual + pltpu.roll(dual, half, 1)
    )
    row1[...] = mine
    r1_cp = [
        send(row1, rows1.at[w], r1_ss.at[d], r1_rs.at[d], there(d, 0)) for d in w_off
    ]
    rows1[w] = mine
    c = CHUNKS - 1
    y1_cp[c] = send_prices(y1, yb1, yo1, y1_ss, y1_rs, c)

    f1_cp = []
    for c in range(CHUNKS):
        mix_arrivals([s1[t, span(c), :] for t in range(ROWS)], fs_1, c)
        f1_cp.append(send_arrivals(fs_1, v1.at[3:4, span(c)], fb_1, fh_1, f1_ss, f1_rs, c))

    for cp in r1_cp:
        cp.wait_recv()
    mine = jnp.sum(rows1[...], axis=0)
    row2[...] = mine
    r2_cp = [
        send(row2, rows2.at[r], r2_ss.at[d], r2_rs.at[d], there(0, d)) for d in range(1, regions)
    ]
    rows2[r] = mine

    for c in range(CHUNKS):
        for cp in y1_cp[c]:
            cp.wait_recv()
        grad_v, grad_s = pulled_gradients(y1, yb1, yo1, c)
        for t in range(ROWS):
            ch[t, span(c), :] = ch[t, span(c), :] - grad_v[t]
            cs[t, span(c), :] = cs[t, span(c), :] - grad_s[t]

    for cp in r2_cp:
        cp.wait_recv()
    total = jnp.sum(rows2[...], axis=0)
    moved_primal = jnp.sum(jnp.where(lane < half, total, 0.0), axis=1, keepdims=True)
    moved_dual = jnp.sum(jnp.where(lane < half, 0.0, total), axis=1, keepdims=True)
    ratio = jnp.broadcast_to((moved_dual + EPS_MOVE) / (moved_primal + EPS_MOVE), (1, PANEL))
    weight = jnp.sqrt(jnp.sqrt(ratio))
    primal_step = STEP_ETA / weight
    dual_step = STEP_ETA * weight

    m_cp = []
    for c in range(CHUNKS):
        sums = jnp.zeros((size, PANEL), F32)
        for t in range(ROWS):
            v2[t, span(c), :] = jnp.maximum(v1[t, span(c), :] - primal_step * ch[t, span(c), :], 0.0)
            new_s = jnp.minimum(
                jnp.maximum(s1[t, span(c), :] - primal_step * cs[t, span(c), :], 0.0),
                cap[t, span(c), :].astype(F32),
            )
            s2[t, span(c), :] = new_s
            sums = sums + new_s
        s_sum[span(c), :] = sums
        m_send[span(c), :] = mix(sums, w_fwd)
        m_cp.append(
            send(m_send.at[span(c)], m_recv.at[span(c)], m_ss.at[c], m_rs.at[c], there(0, 1))
        )
    outs = [
        pltpu.make_async_copy(v2, stock_out, out_sem.at[0]),
        pltpu.make_async_copy(s2, ship_out, out_sem.at[1]),
    ]
    for cp in outs:
        cp.start()

    f2_cp = []

    def last_arrivals(c):
        mix_arrivals([s2[t, span(c), :] for t in range(ROWS)], fs_2, c)
        f2_cp.append(send_arrivals(fs_2, v2.at[3:4, span(c)], fb_2, fh_2, f2_ss, f2_rs, c))

    for c in range(CHUNKS):
        last_arrivals(c)

    for c in range(CHUNKS):
        m_cp[c].wait_recv()
        sums = m_recv[span(c), :] - s_sum[span(c), :]
        for t in range(ROWS):
            sums = sums - dem[t, span(c), :]
        net[span(c), :] = sums
    p1_cp = []
    for d in w_off:
        to = there(d, 0)
        p1_cp.append(
            send(net.at[pl.ds(to[0] * piece, piece)], a1.at[w], p1_ss.at[d], p1_rs.at[d], to)
        )
    a1[w] = net[pl.ds(w * piece, piece), :]

    for c in range(CHUNKS):
        for cp in f1_cp[c]:
            cp.wait_recv()
        _, receipts = arrivals(fb_1, c)
        v_rows = [v1[t, span(c), :] for t in range(ROWS)]
        s_rows = [s1[t, span(c), :] for t in range(ROWS)]
        rows = balance_of(v_rows, s_rows, fh_1, receipts, c)
        for t in range(ROWS):
            bal1[t, span(c), :] = rows[t]

    for cp in p1_cp:
        cp.wait_recv()
    running = jnp.zeros((piece, PANEL), F32)
    for k in range(weeks):
        a2[k] = running
        running = running + a1[k]
    p2_cp = []
    for d in w_off:
        to = there(d, 0)
        p2_cp.append(
            send(a2.at[to[0]], pref.at[pl.ds(w * piece, piece)], p2_ss.at[d], p2_rs.at[d], to)
        )
    pref[pl.ds(w * piece, piece), :] = a2[w]

    for c in range(CHUNKS):
        for cp in f2_cp[c]:
            cp.wait_recv()
        early, receipts = arrivals(fb_2, c)
        v_rows = [v2[t, span(c), :] for t in range(ROWS)]
        s_rows = [s2[t, span(c), :] for t in range(ROWS)]
        rows = balance_of(v_rows, s_rows, fh_2, receipts, c)
        flow = -early[0] - early[1]
        for t in range(ROWS):
            wanted = dem[t, span(c), :]
            y2[t, span(c), :] = y1[t, span(c), :] + dual_step * (
                wanted - 2.0 * rows[t] + bal1[t, span(c), :]
            )
            flow = flow + (receipts[t] - s_rows[t] - wanted)
            pj[t, span(c), :] = flow
    outs.append(pltpu.make_async_copy(y2, dual_out, out_sem.at[2]))
    outs[-1].start()

    for cp in p2_cp:
        cp.wait_recv()
    for t in range(ROWS):
        pj[t] = pj[t] + pref[...]
    outs.append(pltpu.make_async_copy(pj, proj_out, out_sem.at[3]))
    outs[-1].start()
    for cp in sends:
        cp.wait_send()
    for cp in outs:
        cp.wait()


def shards(weeks, regions, stock, ship, dual, demand, hold, cost, cap, lead, mix):
    items = stock.shape[-1]
    panels = items // PANEL

    def view(a):
        return a.reshape(ROWS, panels, PANEL)

    slab = (ROWS, panels, PANEL)

    def vmem(*shape, dtype=F32):
        return pltpu.VMEM(shape, dtype)

    def sems(n):
        return [pltpu.SemaphoreType.DMA((n,))] * 2

    exchange = [vmem(5, panels, PANEL), vmem(5, panels, PANEL), vmem(1, panels, PANEL)]
    scratch = (
        [vmem(*slab)] * 6
        + [vmem(*slab, dtype=jnp.int32), vmem(panels, PANEL, dtype=jnp.int32), vmem(PANEL, PANEL)]
        + [vmem(2 * PANEL, 2 * PANEL, dtype=BF16)] * 2
        + [vmem(*slab)] * 8
        + [vmem(5, panels, PANEL), vmem(1, panels, PANEL)] * 2
        + [vmem(5, panels, PANEL), vmem(1, panels, PANEL)] * 2
        + exchange
        + exchange
        + [vmem(panels, PANEL)] * 4
        + [vmem(weeks, panels // weeks, PANEL)] * 2
        + [vmem(panels, PANEL)]
        + [vmem(1, PANEL), vmem(weeks, 1, PANEL), vmem(1, PANEL), vmem(regions, 1, PANEL)]
        + [pltpu.SemaphoreType.DMA((9,)), pltpu.SemaphoreType.DMA((4,))]
        + sems(3 * CHUNKS) * 5
        + sems(CHUNKS)
        + sems(weeks)
        + sems(regions)
        + sems(weeks) * 2
    )
    outs = pl.pallas_call(
        functools.partial(kernel, weeks, regions, panels),
        out_shape=[jax.ShapeDtypeStruct(slab, F32)] * 4,
        in_specs=[pl.BlockSpec(memory_space=pl.ANY)] * 9,
        out_specs=[pl.BlockSpec(memory_space=pl.ANY)] * 4,
        scratch_shapes=scratch,
        compiler_params=pltpu.CompilerParams(
            collective_id=0, has_side_effects=True, vmem_limit_bytes=48 * 1024 * 1024
        ),
        cost_estimate=pl.CostEstimate(
            flops=2 * 6 * 5 * 5 * panels * PANEL * PANEL,
            bytes_accessed=12 * 4 * ROWS * panels * PANEL,
            transcendentals=0,
        ),
        name="primal_dual",
    )(
        view(stock), view(ship), view(dual), view(demand), view(hold), view(cost), view(cap),
        lead.reshape(panels, PANEL), mix.reshape(PANEL, PANEL),
    )
    return tuple(o.reshape(ROWS, 1, items) for o in outs)


def solution(mesh):
    block = P("week", "region", None)
    in_specs = (block,) * 7 + (P("region", None), P("region", None, None))
    body = functools.partial(shards, mesh.shape["week"], mesh.shape["region"])
    return jax.shard_map(
        body, mesh=mesh, in_specs=in_specs, out_specs=(block,) * 4, check_vma=False
    )
```

```python
import functools

import jax
import jax.numpy as jnp
from jax import lax
from jax.experimental import pallas as pl
from jax.experimental.pallas import tpu as pltpu
from jax.sharding import PartitionSpec as P

PANEL = 128
ROWS = 4
CHUNKS = 4
LAG = 2
STEP_ETA = 0.25
EPS_MOVE = 1e-06
MESH = pl.DeviceIdType.MESH
F32 = jnp.float32
BF16 = jnp.bfloat16


def ring_distance(d, n):
    return min(d % n, -d % n)


def week_offsets(weeks):
    def hops(d):
        return ring_distance(d // 4, max(weeks // 4, 1)) + ring_distance(d % 4, 4)

    return sorted(range(1, weeks), key=lambda d: (-hops(d), d))


def kernel(weeks, regions, panels, *refs):
    (
        stock_in, ship_in, dual_in, demand_in, hold_in, cost_in, cap_in, lead_in, mix_in,
        v2, s2, y2, pj, pref,
        v0, s0, y0, dem, ch, cs, cap, lead, mixw,
        w_fwd, w_adj,
        v1, s1, y1, bal1,
        yb0, yo0, yb1, yo1,
        fs_t, fv_t, fb_t, fh_t,
        fs_1, fb_1, fh_1,
        fs_2, fb_2, fh_2,
        m_send, m_recv, s_sum, net, a1, a2,
        row1, rows1, row2, rows2,
        load_sem,
        y0_ss, y0_rs, y1_ss, y1_rs, ft_ss, ft_rs, f1_ss, f1_rs, f2_ss, f2_rs,
        m_ss, m_rs, r1_ss, r1_rs, r2_ss, r2_rs, p1_ss, p1_rs, p2_ss, p2_rs,
    ) = refs
    w = lax.axis_index("week")
    r = lax.axis_index("region")
    first = w == 0
    last = w == weeks - 1
    size = panels // CHUNKS
    piece = panels // weeks

    def there(dw, dr):
        return (lax.rem(w + dw + weeks, weeks), lax.rem(r + dr + regions, regions))

    loads = []
    for k, (src, dst) in enumerate(
        (
            (dual_in, y0), (mix_in, mixw), (lead_in, lead), (ship_in, s0), (stock_in, v0),
            (hold_in, ch), (cost_in, cs), (cap_in, cap), (demand_in, dem),
        )
    ):
        cp = pltpu.make_async_copy(src, dst, load_sem.at[k])
        cp.start()
        loads.append(cp)

    w_off = week_offsets(weeks)
    near = [(0, 1), (1, 1), (1, 0), (0, -1), (-1, -1), (-1, 0)]
    far = [(d, 0) for d in w_off] + [(0, d) for d in range(1, regions)]
    partners = list(dict.fromkeys((a % weeks, b % regions) for a, b in near + far))
    barrier = pltpu.get_barrier_semaphore()
    for dw, dr in partners:
        pl.semaphore_signal(barrier, inc=1, device_id=there(dw, dr), device_id_type=MESH)
    sends = []

    def send(src, dst, ss, rs, to):
        cp = pltpu.make_async_remote_copy(
            src_ref=src, dst_ref=dst, send_sem=ss, recv_sem=rs, device_id=to, device_id_type=MESH
        )
        cp.start()
        sends.append(cp)
        return cp

    def span(c):
        return pl.ds(c * size, size)

    def send_prices(y, yb, yo, ss, rs, c):
        k = 3 * c
        return [
            send(y.at[0:2, span(c)], yb.at[3:5, span(c)], ss.at[k], rs.at[k], there(-1, -1)),
            send(y.at[0:1, span(c)], yo.at[:, span(c)], ss.at[k + 1], rs.at[k + 1], there(-1, 0)),
            send(y.at[1:4, span(c)], yb.at[0:3, span(c)], ss.at[k + 2], rs.at[k + 2], there(0, -1)),
        ]

    def send_arrivals(fs, fv, fb, fh, ss, rs, c):
        k = 3 * c
        return [
            send(fs.at[3:5, span(c)], fb.at[3:5, span(c)], ss.at[k], rs.at[k], there(1, 1)),
            send(fv, fh.at[:, span(c)], ss.at[k + 1], rs.at[k + 1], there(1, 0)),
            send(fs.at[0:3, span(c)], fb.at[0:3, span(c)], ss.at[k + 2], rs.at[k + 2], there(0, 1)),
        ]

    def mix(values, weight):
        hi = values.astype(BF16)
        lo = (values - hi.astype(F32)).astype(BF16)
        both = jnp.dot(jnp.concatenate([hi, lo], axis=1), weight[...], preferred_element_type=F32)
        return both[:, :PANEL] + both[:, PANEL:]

    def pulled_gradients(y, yb, yo, c):
        pulled = mix(yb[:, span(c), :].reshape(5 * size, PANEL), w_adj).reshape(5, size, PANEL)
        pulled = [pulled[k] for k in range(5)]
        pulled[3] = jnp.where(last, 0.0, pulled[3])
        pulled[4] = jnp.where(last, 0.0, pulled[4])
        short = lead[span(c), :] == 1
        rows = [y[t, span(c), :] for t in range(ROWS)]
        after = rows[1:] + [jnp.where(last, 0.0, yo[0, span(c), :])]
        grad_v = [rows[t] - after[t] for t in range(ROWS)]
        grad_s = [rows[t] - jnp.where(short, pulled[t], pulled[t + 1]) for t in range(ROWS)]
        return grad_v, grad_s

    def mix_arrivals(rows, fs, c):
        short = lead[span(c), :] == 1
        lagged = jnp.concatenate(
            [
                jnp.where(short, rows[0], 0.0),
                jnp.where(short, rows[1], rows[0]),
                jnp.where(short, rows[2], rows[1]),
                jnp.where(short, rows[3], rows[2]),
                jnp.where(short, 0.0, rows[3]),
            ],
            axis=0,
        )
        fs[:, span(c), :] = mix(lagged, w_fwd).reshape(5, size, PANEL)

    def arrivals(fb, c):
        early = [jnp.where(first, 0.0, fb[3 + k, span(c), :]) for k in range(2)]
        own = [fb[k, span(c), :] for k in range(3)]
        return early, [early[0], own[0] + early[1], own[1], own[2]]

    def balance_of(v_rows, s_rows, fh, receipts, c):
        before = [jnp.where(first, 0.0, fh[0, span(c), :])] + v_rows[:-1]
        return [v_rows[t] - before[t] + s_rows[t] - receipts[t] for t in range(ROWS)]

    def fold(values):
        return jnp.sum(values.reshape(size // 8, 8, PANEL), axis=0)

    loads[1].wait()
    for weight, dest in ((mixw[...], w_fwd), (mixw[...].T, w_adj)):
        hi = weight.astype(BF16)
        lo = (weight - hi.astype(F32)).astype(BF16)
        half = jnp.concatenate([hi, lo], axis=1)
        dest[...] = jnp.concatenate([half, half], axis=0)
    f1_cp = {}
    for cp in loads[2:5]:
        cp.wait()
    for c in range(CHUNKS):
        mix_arrivals([s0[t, span(c), :] for t in range(ROWS)], fs_1, c)
    loads[0].wait()

    def send_start(c):
        f1_cp[c] = send_arrivals(fs_1, v0.at[3:4, span(c)], fb_1, fh_1, f1_ss, f1_rs, c)

    pl.semaphore_wait(barrier, len(partners))

    y0_cp = [send_prices(y0, yb0, yo0, y0_ss, y0_rs, c) for c in range(CHUNKS)]
    for c in range(CHUNKS // 2):
        send_start(c)
    for cp in loads[5:]:
        cp.wait()

    primal = jnp.zeros((8, PANEL), F32)
    dual = jnp.zeros((8, PANEL), F32)
    ft_cp = {}
    y1_cp = {}

    def first_primal(c, primal):
        for cp in y0_cp[c]:
            cp.wait_recv()
        grad_v, grad_s = pulled_gradients(y0, yb0, yo0, c)
        ahead = []
        for t in range(ROWS):
            old_v = v0[t, span(c), :]
            new_v = jnp.maximum(old_v - STEP_ETA * (ch[t, span(c), :] - grad_v[t]), 0.0)
            v1[t, span(c), :] = new_v
            if t == ROWS - 1:
                fv_t[0, span(c), :] = 2.0 * new_v - old_v
            old_s = s0[t, span(c), :]
            top = cap[t, span(c), :].astype(F32)
            new_s = jnp.minimum(
                jnp.maximum(old_s - STEP_ETA * (cs[t, span(c), :] - grad_s[t]), 0.0), top
            )
            s1[t, span(c), :] = new_s
            primal = primal + fold((new_v - old_v) ** 2) + fold((new_s - old_s) ** 2)
            ahead.append(2.0 * new_s - old_s)
        mix_arrivals(ahead, fs_t, c)
        ft_cp[c] = send_arrivals(fs_t, fv_t.at[:, span(c)], fb_t, fh_t, ft_ss, ft_rs, c)
        return primal

    def first_dual(c, dual):
        for cp in ft_cp[c]:
            cp.wait_recv()
        _, receipts = arrivals(fb_t, c)
        v_rows = [2.0 * v1[t, span(c), :] - v0[t, span(c), :] for t in range(ROWS)]
        s_rows = [2.0 * s1[t, span(c), :] - s0[t, span(c), :] for t in range(ROWS)]
        ahead = balance_of(v_rows, s_rows, fh_t, receipts, c)
        for t in range(ROWS):
            bal1[t, span(c), :] = ahead[t]
            moved = STEP_ETA * (dem[t, span(c), :] - ahead[t])
            new_y = y0[t, span(c), :] + moved
            y1[t, span(c), :] = new_y
            dual = dual + fold((new_y - y0[t, span(c), :]) ** 2)
        if c < CHUNKS - 1:
            y1_cp[c] = send_prices(y1, yb1, yo1, y1_ss, y1_rs, c)
        return dual

    for c in range(CHUNKS + LAG):
        if c < CHUNKS:
            primal = first_primal(c, primal)
        if c == CHUNKS - 1:
            for k in range(CHUNKS // 2, CHUNKS):
                send_start(k)
        if c >= LAG:
            dual = first_dual(c - LAG, dual)

    lane = lax.broadcasted_iota(jnp.int32, (1, PANEL), 1)
    primal = jnp.sum(primal, axis=0, keepdims=True)
    dual = jnp.sum(dual, axis=0, keepdims=True)
    half = PANEL // 2
    mine = jnp.where(
        lane < half, primal + pltpu.roll(primal, half, 1), dual + pltpu.roll(dual, half, 1)
    )
    row1[...] = mine
    r1_cp = [
        send(row1, rows1.at[w], r1_ss.at[d], r1_rs.at[d], there(d, 0)) for d in w_off
    ]
    rows1[w] = mine
    c = CHUNKS - 1
    y1_cp[c] = send_prices(y1, yb1, yo1, y1_ss, y1_rs, c)

    for cp in r1_cp:
        cp.wait_recv()
    mine = jnp.sum(rows1[...], axis=0)
    row2[...] = mine
    r2_cp = [
        send(row2, rows2.at[r], r2_ss.at[d], r2_rs.at[d], there(0, d)) for d in range(1, regions)
    ]
    rows2[r] = mine

    for c in range(CHUNKS):
        for cp in y1_cp[c]:
            cp.wait_recv()
        grad_v, grad_s = pulled_gradients(y1, yb1, yo1, c)
        for t in range(ROWS):
            ch[t, span(c), :] = ch[t, span(c), :] - grad_v[t]
            cs[t, span(c), :] = cs[t, span(c), :] - grad_s[t]

    for cp in r2_cp:
        cp.wait_recv()
    total = jnp.sum(rows2[...], axis=0)
    moved_primal = jnp.sum(jnp.where(lane < half, total, 0.0), axis=1, keepdims=True)
    moved_dual = jnp.sum(jnp.where(lane < half, 0.0, total), axis=1, keepdims=True)
    ratio = jnp.broadcast_to((moved_dual + EPS_MOVE) / (moved_primal + EPS_MOVE), (1, PANEL))
    weight = jnp.sqrt(jnp.sqrt(ratio))
    primal_step = STEP_ETA / weight
    dual_step = STEP_ETA * weight

    m_cp = []
    for c in range(CHUNKS):
        sums = jnp.zeros((size, PANEL), F32)
        for t in range(ROWS):
            v2[t, span(c), :] = jnp.maximum(v1[t, span(c), :] - primal_step * ch[t, span(c), :], 0.0)
            new_s = jnp.minimum(
                jnp.maximum(s1[t, span(c), :] - primal_step * cs[t, span(c), :], 0.0),
                cap[t, span(c), :].astype(F32),
            )
            s2[t, span(c), :] = new_s
            sums = sums + new_s
        s_sum[span(c), :] = sums
        m_send[span(c), :] = mix(sums, w_fwd)
        m_cp.append(
            send(m_send.at[span(c)], m_recv.at[span(c)], m_ss.at[c], m_rs.at[c], there(0, 1))
        )
    f2_cp = []

    def last_arrivals(c):
        mix_arrivals([s2[t, span(c), :] for t in range(ROWS)], fs_2, c)
        f2_cp.append(send_arrivals(fs_2, v2.at[3:4, span(c)], fb_2, fh_2, f2_ss, f2_rs, c))

    for c in range(CHUNKS):
        last_arrivals(c)

    for c in range(CHUNKS):
        m_cp[c].wait_recv()
        sums = m_recv[span(c), :] - s_sum[span(c), :]
        for t in range(ROWS):
            sums = sums - dem[t, span(c), :]
        net[span(c), :] = sums
    p1_cp = []
    for d in w_off:
        to = there(d, 0)
        p1_cp.append(
            send(net.at[pl.ds(to[0] * piece, piece)], a1.at[w], p1_ss.at[d], p1_rs.at[d], to)
        )
    a1[w] = net[pl.ds(w * piece, piece), :]

    for c in range(CHUNKS):
        for cp in f1_cp[c]:
            cp.wait_recv()
        _, receipts = arrivals(fb_1, c)
        v_rows = [v0[t, span(c), :] for t in range(ROWS)]
        s_rows = [s0[t, span(c), :] for t in range(ROWS)]
        rows = balance_of(v_rows, s_rows, fh_1, receipts, c)
        for t in range(ROWS):
            bal1[t, span(c), :] = 0.5 * (bal1[t, span(c), :] + rows[t])

    for cp in p1_cp:
        cp.wait_recv()
    running = jnp.zeros((piece, PANEL), F32)
    for k in range(weeks):
        a2[k] = running
        running = running + a1[k]
    p2_cp = []
    for d in w_off:
        to = there(d, 0)
        p2_cp.append(
            send(a2.at[to[0]], pref.at[pl.ds(w * piece, piece)], p2_ss.at[d], p2_rs.at[d], to)
        )
    pref[pl.ds(w * piece, piece), :] = a2[w]

    for c in range(CHUNKS):
        for cp in f2_cp[c]:
            cp.wait_recv()
        early, receipts = arrivals(fb_2, c)
        v_rows = [v2[t, span(c), :] for t in range(ROWS)]
        s_rows = [s2[t, span(c), :] for t in range(ROWS)]
        rows = balance_of(v_rows, s_rows, fh_2, receipts, c)
        flow = -early[0] - early[1]
        for t in range(ROWS):
            wanted = dem[t, span(c), :]
            y2[t, span(c), :] = y1[t, span(c), :] + dual_step * (
                wanted - 2.0 * rows[t] + bal1[t, span(c), :]
            )
            flow = flow + (receipts[t] - s_rows[t] - wanted)
            pj[t, span(c), :] = flow
    for cp in p2_cp:
        cp.wait_recv()
    for cp in sends:
        cp.wait_send()


def finish(v2, s2, y2, pj, pref, stock_out, ship_out, dual_out, proj_out, total, sem):
    copies = []
    for k, (src, dst) in enumerate(((v2, stock_out), (s2, ship_out), (y2, dual_out))):
        copies.append(pltpu.make_async_copy(src, dst, sem.at[k]))
        copies[-1].start()
    for t in range(ROWS):
        total[t] = pj[t] + pref[...]
        copies.append(pltpu.make_async_copy(total.at[t], proj_out.at[t], sem.at[3 + t]))
        copies[-1].start()
    for cp in copies:
        cp.wait()


def shards(weeks, regions, stock, ship, dual, demand, hold, cost, cap, lead, mix):
    items = stock.shape[-1]
    panels = items // PANEL

    def in_hbm(a, *shape):
        return pltpu.with_memory_space_constraint(a.reshape(shape), pltpu.HBM)

    def view(a):
        return in_hbm(a, ROWS, panels, PANEL)

    slab = (ROWS, panels, PANEL)

    def vmem(*shape, dtype=F32):
        return pltpu.VMEM(shape, dtype)

    def sems(n):
        return [pltpu.SemaphoreType.DMA((n,))] * 2

    exchange = [vmem(5, panels, PANEL), vmem(5, panels, PANEL), vmem(1, panels, PANEL)]
    scratch = (
        [vmem(*slab)] * 6
        + [vmem(*slab, dtype=jnp.int32), vmem(panels, PANEL, dtype=jnp.int32), vmem(PANEL, PANEL)]
        + [vmem(2 * PANEL, 2 * PANEL, dtype=BF16)] * 2
        + [vmem(*slab)] * 4
        + [vmem(5, panels, PANEL), vmem(1, panels, PANEL)] * 2
        + [vmem(5, panels, PANEL), vmem(1, panels, PANEL)] * 2
        + exchange
        + exchange
        + [vmem(panels, PANEL)] * 4
        + [vmem(weeks, panels // weeks, PANEL)] * 2
        + [vmem(1, PANEL), vmem(weeks, 1, PANEL), vmem(1, PANEL), vmem(regions, 1, PANEL)]
        + [pltpu.SemaphoreType.DMA((9,))]
        + sems(3 * CHUNKS) * 5
        + sems(CHUNKS)
        + sems(weeks)
        + sems(regions)
        + sems(weeks) * 2
    )
    parts = pl.pallas_call(
        functools.partial(kernel, weeks, regions, panels),
        out_shape=[jax.ShapeDtypeStruct(slab, F32)] * 4
        + [jax.ShapeDtypeStruct((panels, PANEL), F32)],
        in_specs=[pl.BlockSpec(memory_space=pltpu.HBM)] * 9,
        out_specs=[pl.BlockSpec(memory_space=pltpu.VMEM)] * 5,
        scratch_shapes=scratch,
        compiler_params=pltpu.CompilerParams(
            collective_id=0, has_side_effects=True, vmem_limit_bytes=40 * 1024 * 1024
        ),
        cost_estimate=pl.CostEstimate(
            flops=2 * 6 * 5 * 5 * panels * PANEL * PANEL,
            bytes_accessed=12 * 4 * ROWS * panels * PANEL,
            transcendentals=0,
        ),
        name="primal_dual",
    )(
        view(stock), view(ship), view(dual), view(demand), view(hold), view(cost), view(cap),
        in_hbm(lead, panels, PANEL), in_hbm(mix, PANEL, PANEL),
    )
    outs = pl.pallas_call(
        finish,
        out_shape=[jax.ShapeDtypeStruct(slab, F32)] * 4,
        in_specs=[pl.BlockSpec(memory_space=pltpu.VMEM)] * 5,
        out_specs=[pl.BlockSpec(memory_space=pltpu.HBM)] * 4,
        scratch_shapes=[vmem(*slab), pltpu.SemaphoreType.DMA((3 + ROWS,))],
        compiler_params=pltpu.CompilerParams(vmem_limit_bytes=8 * 1024 * 1024),
        name="finish",
    )(*parts)
    return tuple(o.reshape(ROWS, 1, items) for o in outs)


def solution(mesh):
    block = P("week", "region", None)
    in_specs = (block,) * 7 + (P("region", None), P("region", None, None))
    body = functools.partial(shards, mesh.shape["week"], mesh.shape["region"])
    return jax.shard_map(
        body, mesh=mesh, in_specs=in_specs, out_specs=(block,) * 4, check_vma=False
    )
```

```python
import functools

import jax
import jax.numpy as jnp
from jax import lax
from jax.experimental import pallas as pl
from jax.experimental.pallas import tpu as pltpu
from jax.sharding import PartitionSpec as P

PANEL = 128
ROWS = 4
SHARES = (8, 8, 7, 6, 3)
CHUNKS = len(SHARES)
LAG = 2
STEP_ETA = 0.25
EPS_MOVE = 1e-06
MESH = pl.DeviceIdType.MESH
F32 = jnp.float32
BF16 = jnp.bfloat16


def ring_distance(d, n):
    return min(d % n, -d % n)


def week_offsets(weeks):
    def hops(d):
        return ring_distance(d // 4, max(weeks // 4, 1)) + ring_distance(d % 4, 4)

    return sorted(range(1, weeks), key=lambda d: (-hops(d), d))


def kernel(weeks, regions, panels, *refs):
    (
        stock_in, ship_in, dual_in, demand_in, hold_in, cost_in, cap_in, lead_in, mix_in,
        v2, s2, y2, pj, pref,
        v0, s0, y0, dem, ch, cs, cap, lead, mixw,
        w_fwd, w_adj,
        v1, s1, y1, bal1,
        yb0, yb1,
        fs_t, fv_t, fb_t,
        fs_1, fb_1,
        fs_2, fb_2,
        m_send, m_recv, s_sum, net, a1, a2,
        row1, rows1, row2, rows2,
        load_sem, send_sem, wide_sem,
        y0_rs, y1_rs, ft_rs, f1_rs, f2_rs, m_rs,
    ) = refs
    w = lax.axis_index("week")
    r = lax.axis_index("region")
    first = w == 0
    last = w == weeks - 1
    sizes = [panels * k // sum(SHARES) for k in SHARES]
    starts = [sum(sizes[:c]) for c in range(CHUNKS)]
    piece = panels // weeks

    def there(dw, dr):
        return (lax.rem(w + dw + weeks, weeks), lax.rem(r + dr + regions, regions))

    loads = []
    for k, (src, dst) in enumerate(
        (
            (dual_in, y0), (mix_in, mixw), (lead_in, lead), (ship_in, s0), (stock_in, v0),
            (hold_in, ch), (cost_in, cs), (cap_in, cap), (demand_in, dem),
        )
    ):
        cp = pltpu.make_async_copy(src, dst, load_sem.at[k])
        cp.start()
        loads.append(cp)

    w_off = week_offsets(weeks)
    near = [(0, 1), (1, 1), (1, 0), (0, -1), (-1, -1), (-1, 0)]
    far = [(d, 0) for d in w_off] + [(0, d) for d in range(1, regions)]
    partners = list(dict.fromkeys((a % weeks, b % regions) for a, b in near + far))
    barrier = pltpu.get_barrier_semaphore()
    for dw, dr in partners:
        pl.semaphore_signal(barrier, inc=1, device_id=there(dw, dr), device_id_type=MESH)
    def send(src, dst, ss, rs, to):
        pltpu.make_async_remote_copy(
            src_ref=src, dst_ref=dst, send_sem=ss, recv_sem=rs, device_id=to, device_id_type=MESH
        ).start()

    def wait_for(ref, sem):
        pltpu.make_async_copy(ref, ref, sem).wait()

    def span(c):
        return pl.ds(starts[c], sizes[c])

    def send_prices(y, yb, ss, rs, c):
        at = span(c)
        send(y.at[0:2, at], yb.at[3:5, at], ss, rs.at[c], there(-1, -1))
        send(y.at[0:1, at], yb.at[5:6, at], ss, rs.at[c], there(-1, 0))
        send(y.at[1:4, at], yb.at[0:3, at], ss, rs.at[c], there(0, -1))

    def send_arrivals(fs, fv, fb, ss, rs, c):
        at = span(c)
        send(fs.at[3:5, at], fb.at[3:5, at], ss, rs.at[c], there(1, 1))
        send(fv, fb.at[5:6, at], ss, rs.at[c], there(1, 0))
        send(fs.at[0:3, at], fb.at[0:3, at], ss, rs.at[c], there(0, 1))

    def mix(values, weight):
        hi = values.astype(BF16)
        lo = (values - hi.astype(F32)).astype(BF16)
        both = jnp.dot(jnp.concatenate([hi, lo], axis=1), weight[...], preferred_element_type=F32)
        return both[:, :PANEL] + both[:, PANEL:]

    def pulled_gradients(y, yb, c):
        pulled = mix(yb[0:5, span(c), :].reshape(5 * sizes[c], PANEL), w_adj)
        pulled = pulled.reshape(5, sizes[c], PANEL)
        pulled = [pulled[k] for k in range(5)]
        pulled[3] = jnp.where(last, 0.0, pulled[3])
        pulled[4] = jnp.where(last, 0.0, pulled[4])
        short = lead[span(c), :] == 1
        rows = [y[t, span(c), :] for t in range(ROWS)]
        after = rows[1:] + [jnp.where(last, 0.0, yb[5, span(c), :])]
        grad_v = [rows[t] - after[t] for t in range(ROWS)]
        grad_s = [rows[t] - jnp.where(short, pulled[t], pulled[t + 1]) for t in range(ROWS)]
        return grad_v, grad_s

    def mix_arrivals(rows, fs, c):
        short = lead[span(c), :] == 1
        lagged = jnp.concatenate(
            [
                jnp.where(short, rows[0], 0.0),
                jnp.where(short, rows[1], rows[0]),
                jnp.where(short, rows[2], rows[1]),
                jnp.where(short, rows[3], rows[2]),
                jnp.where(short, 0.0, rows[3]),
            ],
            axis=0,
        )
        fs[:, span(c), :] = mix(lagged, w_fwd).reshape(5, sizes[c], PANEL)

    def arrivals(fb, c):
        early = [jnp.where(first, 0.0, fb[3 + k, span(c), :]) for k in range(2)]
        own = [fb[k, span(c), :] for k in range(3)]
        return early, [early[0], own[0] + early[1], own[1], own[2]]

    def balance_of(v_rows, s_rows, fb, receipts, c):
        before = [jnp.where(first, 0.0, fb[5, span(c), :])] + v_rows[:-1]
        return [v_rows[t] - before[t] + s_rows[t] - receipts[t] for t in range(ROWS)]

    def fold(values):
        return jnp.sum(values.reshape(values.shape[0] // 8, 8, PANEL), axis=0)

    loads[1].wait()
    for weight, dest in ((mixw[...], w_fwd), (mixw[...].T, w_adj)):
        hi = weight.astype(BF16)
        lo = (weight - hi.astype(F32)).astype(BF16)
        half = jnp.concatenate([hi, lo], axis=1)
        dest[...] = jnp.concatenate([half, half], axis=0)
    for cp in loads[2:5]:
        cp.wait()
    for c in range(CHUNKS):
        mix_arrivals([s0[t, span(c), :] for t in range(ROWS)], fs_1, c)
    loads[0].wait()

    def send_start(c):
        send_arrivals(fs_1, v0.at[3:4, span(c)], fb_1, send_sem.at[0], f1_rs, c)

    pl.semaphore_wait(barrier, len(partners))

    for c in range(CHUNKS):
        send_prices(y0, yb0, send_sem.at[1], y0_rs, c)
    for c in range(CHUNKS // 2):
        send_start(c)
    for cp in loads[5:]:
        cp.wait()

    primal = jnp.zeros((8, PANEL), F32)
    dual = jnp.zeros((8, PANEL), F32)

    def first_primal(c, primal):
        wait_for(yb0.at[:, span(c)], y0_rs.at[c])
        grad_v, grad_s = pulled_gradients(y0, yb0, c)
        ahead = []
        for t in range(ROWS):
            old_v = v0[t, span(c), :]
            new_v = jnp.maximum(old_v - STEP_ETA * (ch[t, span(c), :] - grad_v[t]), 0.0)
            v1[t, span(c), :] = new_v
            if t == ROWS - 1:
                fv_t[0, span(c), :] = 2.0 * new_v - old_v
            old_s = s0[t, span(c), :]
            top = cap[t, span(c), :].astype(F32)
            new_s = jnp.minimum(
                jnp.maximum(old_s - STEP_ETA * (cs[t, span(c), :] - grad_s[t]), 0.0), top
            )
            s1[t, span(c), :] = new_s
            primal = primal + fold((new_v - old_v) ** 2) + fold((new_s - old_s) ** 2)
            ahead.append(2.0 * new_s - old_s)
        mix_arrivals(ahead, fs_t, c)
        send_arrivals(fs_t, fv_t.at[:, span(c)], fb_t, send_sem.at[2], ft_rs, c)
        return primal

    def first_dual(c, dual):
        wait_for(fb_t.at[:, span(c)], ft_rs.at[c])
        _, receipts = arrivals(fb_t, c)
        v_rows = [2.0 * v1[t, span(c), :] - v0[t, span(c), :] for t in range(ROWS)]
        s_rows = [2.0 * s1[t, span(c), :] - s0[t, span(c), :] for t in range(ROWS)]
        ahead = balance_of(v_rows, s_rows, fb_t, receipts, c)
        for t in range(ROWS):
            bal1[t, span(c), :] = ahead[t]
            moved = STEP_ETA * (dem[t, span(c), :] - ahead[t])
            new_y = y0[t, span(c), :] + moved
            y1[t, span(c), :] = new_y
            dual = dual + fold((new_y - y0[t, span(c), :]) ** 2)
        if c < CHUNKS - 1:
            send_prices(y1, yb1, send_sem.at[3], y1_rs, c)
        return dual

    for c in range(CHUNKS + LAG):
        if c < CHUNKS:
            primal = first_primal(c, primal)
        if c == CHUNKS - 1:
            for k in range(CHUNKS // 2, CHUNKS):
                send_start(k)
        if c >= LAG:
            dual = first_dual(c - LAG, dual)

    lane = lax.broadcasted_iota(jnp.int32, (1, PANEL), 1)
    primal = jnp.sum(primal, axis=0, keepdims=True)
    dual = jnp.sum(dual, axis=0, keepdims=True)
    half = PANEL // 2
    mine = jnp.where(
        lane < half, primal + pltpu.roll(primal, half, 1), dual + pltpu.roll(dual, half, 1)
    )
    row1[...] = mine
    for d in w_off:
        send(row1, rows1.at[w], wide_sem.at[0], wide_sem.at[1], there(d, 0))
    rows1[w] = mine
    send_prices(y1, yb1, send_sem.at[3], y1_rs, CHUNKS - 1)

    wait_for(rows1.at[0 : weeks - 1], wide_sem.at[1])
    mine = jnp.sum(rows1[...], axis=0)
    row2[...] = mine
    for d in range(1, regions):
        send(row2, rows2.at[r], wide_sem.at[2], wide_sem.at[3], there(0, d))
    rows2[r] = mine

    for c in range(CHUNKS):
        wait_for(yb1.at[:, span(c)], y1_rs.at[c])
        grad_v, grad_s = pulled_gradients(y1, yb1, c)
        for t in range(ROWS):
            ch[t, span(c), :] = ch[t, span(c), :] - grad_v[t]
            cs[t, span(c), :] = cs[t, span(c), :] - grad_s[t]

    wait_for(rows2.at[0 : regions - 1], wide_sem.at[3])
    total = jnp.sum(rows2[...], axis=0)
    moved_primal = jnp.sum(jnp.where(lane < half, total, 0.0), axis=1, keepdims=True)
    moved_dual = jnp.sum(jnp.where(lane < half, 0.0, total), axis=1, keepdims=True)
    ratio = jnp.broadcast_to((moved_dual + EPS_MOVE) / (moved_primal + EPS_MOVE), (1, PANEL))
    weight = jnp.sqrt(jnp.sqrt(ratio))
    primal_step = STEP_ETA / weight
    dual_step = STEP_ETA * weight

    for c in range(CHUNKS):
        sums = jnp.zeros((sizes[c], PANEL), F32)
        for t in range(ROWS):
            v2[t, span(c), :] = jnp.maximum(v1[t, span(c), :] - primal_step * ch[t, span(c), :], 0.0)
            new_s = jnp.minimum(
                jnp.maximum(s1[t, span(c), :] - primal_step * cs[t, span(c), :], 0.0),
                cap[t, span(c), :].astype(F32),
            )
            s2[t, span(c), :] = new_s
            sums = sums + new_s
        s_sum[span(c), :] = sums
        m_send[span(c), :] = mix(sums, w_fwd)
        send(m_send.at[span(c)], m_recv.at[span(c)], wide_sem.at[4], m_rs.at[c], there(0, 1))
    for c in range(CHUNKS):
        wait_for(m_recv.at[span(c)], m_rs.at[c])
        sums = m_recv[span(c), :] - s_sum[span(c), :]
        for t in range(ROWS):
            sums = sums - dem[t, span(c), :]
        net[span(c), :] = sums
    for d in w_off:
        to = there(d, 0)
        send(net.at[pl.ds(to[0] * piece, piece)], a1.at[w], wide_sem.at[5], wide_sem.at[6], to)
    a1[w] = net[pl.ds(w * piece, piece), :]

    for c in range(CHUNKS):
        mix_arrivals([s2[t, span(c), :] for t in range(ROWS)], fs_2, c)
        send_arrivals(fs_2, v2.at[3:4, span(c)], fb_2, send_sem.at[4], f2_rs, c)

    for c in range(CHUNKS):
        wait_for(fb_1.at[:, span(c)], f1_rs.at[c])
        _, receipts = arrivals(fb_1, c)
        v_rows = [v0[t, span(c), :] for t in range(ROWS)]
        s_rows = [s0[t, span(c), :] for t in range(ROWS)]
        rows = balance_of(v_rows, s_rows, fb_1, receipts, c)
        for t in range(ROWS):
            bal1[t, span(c), :] = 0.5 * (bal1[t, span(c), :] + rows[t])

    wait_for(a1.at[0 : weeks - 1], wide_sem.at[6])
    running = jnp.zeros((piece, PANEL), F32)
    for k in range(weeks):
        a2[k] = running
        running = running + a1[k]
    for d in w_off:
        to = there(d, 0)
        send(a2.at[to[0]], pref.at[pl.ds(w * piece, piece)], wide_sem.at[7], wide_sem.at[8], to)
    pref[pl.ds(w * piece, piece), :] = a2[w]

    for c in range(CHUNKS):
        wait_for(fb_2.at[:, span(c)], f2_rs.at[c])
        early, receipts = arrivals(fb_2, c)
        v_rows = [v2[t, span(c), :] for t in range(ROWS)]
        s_rows = [s2[t, span(c), :] for t in range(ROWS)]
        rows = balance_of(v_rows, s_rows, fb_2, receipts, c)
        flow = -early[0] - early[1]
        for t in range(ROWS):
            wanted = dem[t, span(c), :]
            y2[t, span(c), :] = y1[t, span(c), :] + dual_step * (
                wanted - 2.0 * rows[t] + bal1[t, span(c), :]
            )
            flow = flow + (receipts[t] - s_rows[t] - wanted)
            pj[t, span(c), :] = flow
    for k, landing in enumerate((fb_1, yb0, fb_t, yb1, fb_2)):
        wait_for(landing, send_sem.at[k])
    wait_for(rows1.at[0 : weeks - 1], wide_sem.at[0])
    wait_for(rows2.at[0 : regions - 1], wide_sem.at[2])
    wait_for(m_recv, wide_sem.at[4])
    wait_for(a1.at[0 : weeks - 1], wide_sem.at[5])
    wait_for(a2.at[0 : weeks - 1], wide_sem.at[7])
    wait_for(pref.at[0 : panels - piece], wide_sem.at[8])


def finish(v2, s2, y2, pj, pref, stock_out, ship_out, dual_out, proj_out, total, sem):
    copies = []
    for k, (src, dst) in enumerate(((v2, stock_out), (s2, ship_out), (y2, dual_out))):
        copies.append(pltpu.make_async_copy(src, dst, sem.at[k]))
        copies[-1].start()
    for t in range(ROWS):
        total[t] = pj[t] + pref[...]
        copies.append(pltpu.make_async_copy(total.at[t], proj_out.at[t], sem.at[3 + t]))
        copies[-1].start()
    for cp in copies:
        cp.wait()


def shards(weeks, regions, stock, ship, dual, demand, hold, cost, cap, lead, mix):
    items = stock.shape[-1]
    panels = items // PANEL

    def in_hbm(a, *shape):
        return pltpu.with_memory_space_constraint(a.reshape(shape), pltpu.HBM)

    def view(a):
        return in_hbm(a, ROWS, panels, PANEL)

    slab = (ROWS, panels, PANEL)

    def vmem(*shape, dtype=F32):
        return pltpu.VMEM(shape, dtype)

    def sems(n):
        return pltpu.SemaphoreType.DMA((n,))

    scratch = (
        [vmem(*slab)] * 6
        + [vmem(*slab, dtype=jnp.int32), vmem(panels, PANEL, dtype=jnp.int32), vmem(PANEL, PANEL)]
        + [vmem(2 * PANEL, 2 * PANEL, dtype=BF16)] * 2
        + [vmem(*slab)] * 4
        + [vmem(6, panels, PANEL)] * 2
        + [vmem(5, panels, PANEL), vmem(1, panels, PANEL), vmem(6, panels, PANEL)]
        + [vmem(5, panels, PANEL), vmem(6, panels, PANEL)] * 2
        + [vmem(panels, PANEL)] * 4
        + [vmem(weeks, panels // weeks, PANEL)] * 2
        + [vmem(1, PANEL), vmem(weeks, 1, PANEL), vmem(1, PANEL), vmem(regions, 1, PANEL)]
        + [sems(9), sems(5), sems(9)]
        + [sems(CHUNKS)] * 6
    )
    parts = pl.pallas_call(
        functools.partial(kernel, weeks, regions, panels),
        out_shape=[jax.ShapeDtypeStruct(slab, F32)] * 4
        + [jax.ShapeDtypeStruct((panels, PANEL), F32)],
        in_specs=[pl.BlockSpec(memory_space=pltpu.HBM)] * 9,
        out_specs=[pl.BlockSpec(memory_space=pltpu.VMEM)] * 5,
        scratch_shapes=scratch,
        compiler_params=pltpu.CompilerParams(
            collective_id=0, has_side_effects=True, vmem_limit_bytes=40 * 1024 * 1024
        ),
        cost_estimate=pl.CostEstimate(
            flops=2 * 6 * 5 * 5 * panels * PANEL * PANEL,
            bytes_accessed=12 * 4 * ROWS * panels * PANEL,
            transcendentals=0,
        ),
        name="primal_dual",
    )(
        view(stock), view(ship), view(dual), view(demand), view(hold), view(cost), view(cap),
        in_hbm(lead, panels, PANEL), in_hbm(mix, PANEL, PANEL),
    )
    outs = pl.pallas_call(
        finish,
        out_shape=[jax.ShapeDtypeStruct(slab, F32)] * 4,
        in_specs=[pl.BlockSpec(memory_space=pltpu.VMEM)] * 5,
        out_specs=[pl.BlockSpec(memory_space=pltpu.HBM)] * 4,
        scratch_shapes=[vmem(*slab), pltpu.SemaphoreType.DMA((3 + ROWS,))],
        compiler_params=pltpu.CompilerParams(vmem_limit_bytes=8 * 1024 * 1024),
        name="finish",
    )(*parts)
    return tuple(o.reshape(ROWS, 1, items) for o in outs)


def solution(mesh):
    block = P("week", "region", None)
    in_specs = (block,) * 7 + (P("region", None), P("region", None, None))
    body = functools.partial(shards, mesh.shape["week"], mesh.shape["region"])
    return jax.shard_map(
        body, mesh=mesh, in_specs=in_specs, out_specs=(block,) * 4, check_vma=False
    )
```

```python
import functools

import jax
import jax.numpy as jnp
from jax import lax
from jax.experimental import pallas as pl
from jax.experimental.pallas import tpu as pltpu
from jax.sharding import PartitionSpec as P

PANEL = 128
ROWS = 4
SHARES = (8, 8, 7, 6, 3)
CHUNKS = len(SHARES)
EARLY = 2
QUARTERS = (2, 1, 3, 0)
LAG = 2
STEP_ETA = 0.25
EPS_MOVE = 1e-06
MESH = pl.DeviceIdType.MESH
F32 = jnp.float32
BF16 = jnp.bfloat16


def ring_distance(d, n):
    return min(d % n, -d % n)


def week_offsets(weeks):
    def hops(d):
        return ring_distance(d // 4, max(weeks // 4, 1)) + ring_distance(d % 4, 4)

    return sorted(range(1, weeks), key=lambda d: (-hops(d), d))


def kernel(weeks, regions, panels, *refs):
    (
        stock_in, ship_in, dual_in, demand_in, hold_in, cost_in, cap_in, lead_in, mix_in,
        v2, s2, y2, pj, pref,
        v0, s0, y0, dem, ch, cs, cap, lead, mixw,
        w_fwd, w_adj,
        v1, s1, y1, bal1,
        yb0, yb1,
        fs_t, fv_t, fb_t,
        fs_1, fb_1,
        fs_2, fb_2,
        m_send, m_recv, s_sum, net, a1, a2,
        row1, rows1, row2, rows2,
        load_sem, send_sem, wide_sem,
        y0_rs, y1_rs, ft_rs, f1_rs, f2_rs, m_rs,
    ) = refs
    w = lax.axis_index("week")
    r = lax.axis_index("region")
    first = w == 0
    last = w == weeks - 1
    sizes = [panels * k // sum(SHARES) for k in SHARES]
    starts = [sum(sizes[:c]) for c in range(CHUNKS)]
    piece = panels // weeks

    def there(dw, dr):
        return (lax.rem(w + dw + weeks, weeks), lax.rem(r + dr + regions, regions))

    loads = []
    for k, (src, dst) in enumerate(
        (
            (dual_in, y0), (mix_in, mixw), (lead_in, lead), (ship_in, s0), (stock_in, v0),
            (hold_in, ch), (cost_in, cs), (cap_in, cap), (demand_in, dem),
        )
    ):
        cp = pltpu.make_async_copy(src, dst, load_sem.at[k])
        cp.start()
        loads.append(cp)

    w_off = week_offsets(weeks)
    near = [(0, 1), (1, 1), (1, 0), (0, -1), (-1, -1), (-1, 0)]
    far = [(d, 0) for d in w_off] + [(0, d) for d in range(1, regions)]
    partners = list(dict.fromkeys((a % weeks, b % regions) for a, b in near + far))
    barrier = pltpu.get_barrier_semaphore()
    for dw, dr in partners:
        pl.semaphore_signal(barrier, inc=1, device_id=there(dw, dr), device_id_type=MESH)
    def send(src, dst, ss, rs, to):
        pltpu.make_async_remote_copy(
            src_ref=src, dst_ref=dst, send_sem=ss, recv_sem=rs, device_id=to, device_id_type=MESH
        ).start()

    def wait_for(ref, sem):
        pltpu.make_async_copy(ref, ref, sem).wait()

    def span(c):
        return pl.ds(starts[c], sizes[c])

    def send_prices(y, yb, ss, rs, c):
        at = span(c)
        send(y.at[0:2, at], yb.at[3:5, at], ss, rs.at[c], there(-1, -1))
        send(y.at[0:1, at], yb.at[5:6, at], ss, rs.at[c], there(-1, 0))
        send(y.at[1:4, at], yb.at[0:3, at], ss, rs.at[c], there(0, -1))

    def send_arrivals(fs, fv, fb, ss, rs, c):
        at = span(c)
        send(fs.at[3:5, at], fb.at[3:5, at], ss, rs.at[c], there(1, 1))
        send(fv, fb.at[5:6, at], ss, rs.at[c], there(1, 0))
        send(fs.at[0:3, at], fb.at[0:3, at], ss, rs.at[c], there(0, 1))

    def mix(values, weight):
        hi = values.astype(BF16)
        lo = (values - hi.astype(F32)).astype(BF16)
        both = jnp.dot(jnp.concatenate([hi, lo], axis=1), weight[...], preferred_element_type=F32)
        return both[:, :PANEL] + both[:, PANEL:]

    def pulled_gradients(y, yb, c):
        pulled = mix(yb[0:5, span(c), :].reshape(5 * sizes[c], PANEL), w_adj)
        pulled = pulled.reshape(5, sizes[c], PANEL)
        pulled = [pulled[k] for k in range(5)]
        pulled[3] = jnp.where(last, 0.0, pulled[3])
        pulled[4] = jnp.where(last, 0.0, pulled[4])
        short = lead[span(c), :] == 1
        rows = [y[t, span(c), :] for t in range(ROWS)]
        after = rows[1:] + [jnp.where(last, 0.0, yb[5, span(c), :])]
        grad_v = [rows[t] - after[t] for t in range(ROWS)]
        grad_s = [rows[t] - jnp.where(short, pulled[t], pulled[t + 1]) for t in range(ROWS)]
        return grad_v, grad_s

    def mix_arrivals(rows, fs, c):
        short = lead[span(c), :] == 1
        lagged = jnp.concatenate(
            [
                jnp.where(short, rows[0], 0.0),
                jnp.where(short, rows[1], rows[0]),
                jnp.where(short, rows[2], rows[1]),
                jnp.where(short, rows[3], rows[2]),
                jnp.where(short, 0.0, rows[3]),
            ],
            axis=0,
        )
        fs[:, span(c), :] = mix(lagged, w_fwd).reshape(5, sizes[c], PANEL)

    def arrivals(fb, c):
        early = [jnp.where(first, 0.0, fb[3 + k, span(c), :]) for k in range(2)]
        own = [fb[k, span(c), :] for k in range(3)]
        return early, [early[0], own[0] + early[1], own[1], own[2]]

    def balance_of(v_rows, s_rows, fb, receipts, c):
        before = [jnp.where(first, 0.0, fb[5, span(c), :])] + v_rows[:-1]
        return [v_rows[t] - before[t] + s_rows[t] - receipts[t] for t in range(ROWS)]

    def fold(values):
        return jnp.sum(values.reshape(values.shape[0] // 8, 8, PANEL), axis=0)

    loads[1].wait()
    for weight, dest in ((mixw[...], w_fwd), (mixw[...].T, w_adj)):
        hi = weight.astype(BF16)
        lo = (weight - hi.astype(F32)).astype(BF16)
        half = jnp.concatenate([hi, lo], axis=1)
        dest[...] = jnp.concatenate([half, half], axis=0)
    for cp in loads[2:5]:
        cp.wait()
    for c in range(CHUNKS):
        mix_arrivals([s0[t, span(c), :] for t in range(ROWS)], fs_1, c)
    loads[0].wait()

    def send_start(c):
        send_arrivals(fs_1, v0.at[3:4, span(c)], fb_1, send_sem.at[0], f1_rs, c)

    pl.semaphore_wait(barrier, len(partners))

    for c in range(CHUNKS):
        send_prices(y0, yb0, send_sem.at[1], y0_rs, c)
    for c in range(CHUNKS // 2):
        send_start(c)
    for cp in loads[5:]:
        cp.wait()

    primal = jnp.zeros((8, PANEL), F32)
    dual = jnp.zeros((8, PANEL), F32)

    def first_primal(c, primal):
        wait_for(yb0.at[:, span(c)], y0_rs.at[c])
        grad_v, grad_s = pulled_gradients(y0, yb0, c)
        ahead = []
        for t in range(ROWS):
            old_v = v0[t, span(c), :]
            new_v = jnp.maximum(old_v - STEP_ETA * (ch[t, span(c), :] - grad_v[t]), 0.0)
            v1[t, span(c), :] = new_v
            if t == ROWS - 1:
                fv_t[0, span(c), :] = 2.0 * new_v - old_v
            old_s = s0[t, span(c), :]
            top = cap[t, span(c), :].astype(F32)
            new_s = jnp.minimum(
                jnp.maximum(old_s - STEP_ETA * (cs[t, span(c), :] - grad_s[t]), 0.0), top
            )
            s1[t, span(c), :] = new_s
            primal = primal + fold((new_v - old_v) ** 2) + fold((new_s - old_s) ** 2)
            ahead.append(2.0 * new_s - old_s)
        mix_arrivals(ahead, fs_t, c)
        send_arrivals(fs_t, fv_t.at[:, span(c)], fb_t, send_sem.at[2], ft_rs, c)
        return primal

    def first_dual(c, dual):
        wait_for(fb_t.at[:, span(c)], ft_rs.at[c])
        _, receipts = arrivals(fb_t, c)
        v_rows = [2.0 * v1[t, span(c), :] - v0[t, span(c), :] for t in range(ROWS)]
        s_rows = [2.0 * s1[t, span(c), :] - s0[t, span(c), :] for t in range(ROWS)]
        ahead = balance_of(v_rows, s_rows, fb_t, receipts, c)
        for t in range(ROWS):
            bal1[t, span(c), :] = ahead[t]
            moved = STEP_ETA * (dem[t, span(c), :] - ahead[t])
            new_y = y0[t, span(c), :] + moved
            y1[t, span(c), :] = new_y
            dual = dual + fold((new_y - y0[t, span(c), :]) ** 2)
        if c < CHUNKS - 1:
            send_prices(y1, yb1, send_sem.at[3], y1_rs, c)
        return dual

    for c in range(CHUNKS + LAG):
        if c < CHUNKS:
            primal = first_primal(c, primal)
        if c == CHUNKS - 1:
            for k in range(CHUNKS // 2, CHUNKS):
                send_start(k)
        if c >= LAG:
            dual = first_dual(c - LAG, dual)

    lane = lax.broadcasted_iota(jnp.int32, (1, PANEL), 1)
    primal = jnp.sum(primal, axis=0, keepdims=True)
    dual = jnp.sum(dual, axis=0, keepdims=True)
    half = PANEL // 2
    mine = jnp.where(
        lane < half, primal + pltpu.roll(primal, half, 1), dual + pltpu.roll(dual, half, 1)
    )
    row1[...] = mine
    for d in w_off:
        send(row1, rows1.at[w], wide_sem.at[0], wide_sem.at[1], there(d, 0))
    rows1[w] = mine
    send_prices(y1, yb1, send_sem.at[3], y1_rs, CHUNKS - 1)

    wait_for(rows1.at[0 : weeks - 1], wide_sem.at[1])
    mine = jnp.sum(rows1[...], axis=0)
    row2[...] = mine
    for d in range(1, regions):
        send(row2, rows2.at[r], wide_sem.at[2], wide_sem.at[3], there(0, d))
    rows2[r] = mine

    for c in range(CHUNKS):
        wait_for(yb1.at[:, span(c)], y1_rs.at[c])
        grad_v, grad_s = pulled_gradients(y1, yb1, c)
        for t in range(ROWS):
            ch[t, span(c), :] = ch[t, span(c), :] - grad_v[t]
            cs[t, span(c), :] = cs[t, span(c), :] - grad_s[t]

    s_sum[...] = dem[0] + dem[1] + dem[2] + dem[3]

    wait_for(rows2.at[0 : regions - 1], wide_sem.at[3])
    total = jnp.sum(rows2[...], axis=0)
    moved_primal = jnp.sum(jnp.where(lane < half, total, 0.0), axis=1, keepdims=True)
    moved_dual = jnp.sum(jnp.where(lane < half, 0.0, total), axis=1, keepdims=True)
    ratio = jnp.broadcast_to((moved_dual + EPS_MOVE) / (moved_primal + EPS_MOVE), (1, PANEL))
    weight = jnp.sqrt(jnp.sqrt(ratio))
    primal_step = STEP_ETA / weight
    dual_step = STEP_ETA * weight

    owners = weeks // 4
    quarter = panels // 4

    def quarter_at(k):
        q = lax.rem(lax.div(w, owners) + k, 4)
        return q, pl.ds(pl.multiple_of(q * quarter, 8), quarter)

    for k in QUARTERS:
        _, at = quarter_at(k)
        sums = jnp.zeros((quarter, PANEL), F32)
        for t in range(ROWS):
            new_s = jnp.minimum(
                jnp.maximum(s1[t, at, :] - primal_step * cs[t, at, :], 0.0), cap[t, at, :].astype(F32)
            )
            s2[t, at, :] = new_s
            sums = sums + new_s
        s_sum[at, :] = s_sum[at, :] + sums
        m_send[at, :] = mix(sums, w_fwd)
        send(m_send.at[at], m_recv.at[at], wide_sem.at[4], m_rs.at[k], there(0, 1))

    def last_arrivals(c):
        for t in range(ROWS):
            v2[t, span(c), :] = jnp.maximum(v1[t, span(c), :] - primal_step * ch[t, span(c), :], 0.0)
        mix_arrivals([s2[t, span(c), :] for t in range(ROWS)], fs_2, c)
        send_arrivals(fs_2, v2.at[3:4, span(c)], fb_2, send_sem.at[4], f2_rs, c)

    for c in range(EARLY):
        last_arrivals(c)

    for k in QUARTERS:
        q, at = quarter_at(k)
        wait_for(m_recv.at[at], m_rs.at[k])
        net[at, :] = m_recv[at, :] - s_sum[at, :]
        for j in range(0 if k else 1, owners):
            to = q * owners + lax.rem(w + j, owners)
            send(net.at[pl.ds(to * piece, piece)], a1.at[w], wide_sem.at[5], wide_sem.at[6], (to, r))
    a1[w] = net[pl.ds(w * piece, piece), :]

    for c in range(EARLY, CHUNKS):
        last_arrivals(c)

    for c in range(CHUNKS):
        wait_for(fb_1.at[:, span(c)], f1_rs.at[c])
        _, receipts = arrivals(fb_1, c)
        v_rows = [v0[t, span(c), :] for t in range(ROWS)]
        s_rows = [s0[t, span(c), :] for t in range(ROWS)]
        rows = balance_of(v_rows, s_rows, fb_1, receipts, c)
        for t in range(ROWS):
            bal1[t, span(c), :] = 0.5 * (bal1[t, span(c), :] + rows[t])

    wait_for(a1.at[0 : weeks - 1], wide_sem.at[6])
    running = jnp.zeros((piece, PANEL), F32)
    for k in range(weeks):
        a2[k] = running
        running = running + a1[k]
    for d in w_off:
        to = there(d, 0)
        send(a2.at[to[0]], pref.at[pl.ds(w * piece, piece)], wide_sem.at[7], wide_sem.at[8], to)
    pref[pl.ds(w * piece, piece), :] = a2[w]

    for c in range(CHUNKS):
        wait_for(fb_2.at[:, span(c)], f2_rs.at[c])
        early, receipts = arrivals(fb_2, c)
        v_rows = [v2[t, span(c), :] for t in range(ROWS)]
        s_rows = [s2[t, span(c), :] for t in range(ROWS)]
        rows = balance_of(v_rows, s_rows, fb_2, receipts, c)
        flow = -early[0] - early[1]
        for t in range(ROWS):
            wanted = dem[t, span(c), :]
            y2[t, span(c), :] = y1[t, span(c), :] + dual_step * (
                wanted - 2.0 * rows[t] + bal1[t, span(c), :]
            )
            flow = flow + (receipts[t] - s_rows[t] - wanted)
            pj[t, span(c), :] = flow
    for k, landing in enumerate((fb_1, yb0, fb_t, yb1, fb_2)):
        wait_for(landing, send_sem.at[k])
    wait_for(rows1.at[0 : weeks - 1], wide_sem.at[0])
    wait_for(rows2.at[0 : regions - 1], wide_sem.at[2])
    wait_for(m_recv, wide_sem.at[4])
    wait_for(a1.at[0 : weeks - 1], wide_sem.at[5])
    wait_for(a2.at[0 : weeks - 1], wide_sem.at[7])
    wait_for(pref.at[0 : panels - piece], wide_sem.at[8])


def finish(v2, s2, y2, pj, pref, stock_out, ship_out, dual_out, proj_out, total, sem):
    copies = []
    for k, (src, dst) in enumerate(((v2, stock_out), (s2, ship_out), (y2, dual_out))):
        copies.append(pltpu.make_async_copy(src, dst, sem.at[k]))
        copies[-1].start()
    for t in range(ROWS):
        total[t] = pj[t] + pref[...]
        copies.append(pltpu.make_async_copy(total.at[t], proj_out.at[t], sem.at[3 + t]))
        copies[-1].start()
    for cp in copies:
        cp.wait()


def shards(weeks, regions, stock, ship, dual, demand, hold, cost, cap, lead, mix):
    items = stock.shape[-1]
    panels = items // PANEL

    def in_hbm(a, *shape):
        return pltpu.with_memory_space_constraint(a.reshape(shape), pltpu.HBM)

    def view(a):
        return in_hbm(a, ROWS, panels, PANEL)

    slab = (ROWS, panels, PANEL)

    def vmem(*shape, dtype=F32):
        return pltpu.VMEM(shape, dtype)

    def sems(n):
        return pltpu.SemaphoreType.DMA((n,))

    scratch = (
        [vmem(*slab)] * 6
        + [vmem(*slab, dtype=jnp.int32), vmem(panels, PANEL, dtype=jnp.int32), vmem(PANEL, PANEL)]
        + [vmem(2 * PANEL, 2 * PANEL, dtype=BF16)] * 2
        + [vmem(*slab)] * 4
        + [vmem(6, panels, PANEL)] * 2
        + [vmem(5, panels, PANEL), vmem(1, panels, PANEL), vmem(6, panels, PANEL)]
        + [vmem(5, panels, PANEL), vmem(6, panels, PANEL)] * 2
        + [vmem(panels, PANEL)] * 4
        + [vmem(weeks, panels // weeks, PANEL)] * 2
        + [vmem(1, PANEL), vmem(weeks, 1, PANEL), vmem(1, PANEL), vmem(regions, 1, PANEL)]
        + [sems(9), sems(5), sems(9)]
        + [sems(CHUNKS)] * 5
        + [sems(4)]
    )
    parts = pl.pallas_call(
        functools.partial(kernel, weeks, regions, panels),
        out_shape=[jax.ShapeDtypeStruct(slab, F32)] * 4
        + [jax.ShapeDtypeStruct((panels, PANEL), F32)],
        in_specs=[pl.BlockSpec(memory_space=pltpu.HBM)] * 9,
        out_specs=[pl.BlockSpec(memory_space=pltpu.VMEM)] * 5,
        scratch_shapes=scratch,
        compiler_params=pltpu.CompilerParams(
            collective_id=0, has_side_effects=True, vmem_limit_bytes=40 * 1024 * 1024
        ),
        cost_estimate=pl.CostEstimate(
            flops=2 * 6 * 5 * 5 * panels * PANEL * PANEL,
            bytes_accessed=12 * 4 * ROWS * panels * PANEL,
            transcendentals=0,
        ),
        name="primal_dual",
    )(
        view(stock), view(ship), view(dual), view(demand), view(hold), view(cost), view(cap),
        in_hbm(lead, panels, PANEL), in_hbm(mix, PANEL, PANEL),
    )
    outs = pl.pallas_call(
        finish,
        out_shape=[jax.ShapeDtypeStruct(slab, F32)] * 4,
        in_specs=[pl.BlockSpec(memory_space=pltpu.VMEM)] * 5,
        out_specs=[pl.BlockSpec(memory_space=pltpu.HBM)] * 4,
        scratch_shapes=[vmem(*slab), pltpu.SemaphoreType.DMA((3 + ROWS,))],
        compiler_params=pltpu.CompilerParams(vmem_limit_bytes=8 * 1024 * 1024),
        name="finish",
    )(*parts)
    return tuple(o.reshape(ROWS, 1, items) for o in outs)


def solution(mesh):
    block = P("week", "region", None)
    in_specs = (block,) * 7 + (P("region", None), P("region", None, None))
    body = functools.partial(shards, mesh.shape["week"], mesh.shape["region"])
    return jax.shard_map(
        body, mesh=mesh, in_specs=in_specs, out_specs=(block,) * 4, check_vma=False
    )
```

```python
import functools

import jax
import jax.numpy as jnp
from jax import lax
from jax.experimental import pallas as pl
from jax.experimental.pallas import tpu as pltpu
from jax.sharding import PartitionSpec as P

PANEL = 128
ROWS = 4
SHARES = (8, 8, 7, 6, 3)
CHUNKS = len(SHARES)
EARLY = 2
QUARTERS = (2, 1, 3, 0)
LAG = 2
STEP_ETA = 0.25
EPS_MOVE = 1e-06
MESH = pl.DeviceIdType.MESH
F32 = jnp.float32
BF16 = jnp.bfloat16


def ring_distance(d, n):
    return min(d % n, -d % n)


def week_offsets(weeks):
    def hops(d):
        return ring_distance(d // 4, max(weeks // 4, 1)) + ring_distance(d % 4, 4)

    return sorted(range(1, weeks), key=lambda d: (-hops(d), d))


def kernel(weeks, regions, panels, *refs):
    (
        stock_in, ship_in, dual_in, demand_in, hold_in, cost_in, cap_in, lead_in, mix_in,
        v2, s2, y2, pj, pref,
        v0, s0, y0, dem, ch, cs, cap, lead, mixw,
        w_fwd, w_adj,
        v1, s1, y1, bal1,
        yb0, yb1,
        fs_t, fv_t, fb_t,
        fs_1, fb_1,
        fs_2, fb_2,
        m_send, m_recv, s_sum, net, a1, a2,
        row1, rows1, row2, rows2,
        load_sem, send_sem, wide_sem, round_sem,
        y0_rs, y1_rs, ft_rs, f1_rs, f2_rs, m_rs,
    ) = refs
    w = lax.axis_index("week")
    r = lax.axis_index("region")
    first = w == 0
    last = w == weeks - 1
    sizes = [panels * k // sum(SHARES) for k in SHARES]
    starts = [sum(sizes[:c]) for c in range(CHUNKS)]
    piece = panels // weeks

    def there(dw, dr):
        return (lax.rem(w + dw + weeks, weeks), lax.rem(r + dr + regions, regions))

    loads = []
    for k, (src, dst) in enumerate(
        (
            (dual_in, y0), (mix_in, mixw), (lead_in, lead), (ship_in, s0), (stock_in, v0),
            (hold_in, ch), (cost_in, cs), (cap_in, cap), (demand_in, dem),
        )
    ):
        cp = pltpu.make_async_copy(src, dst, load_sem.at[k])
        cp.start()
        loads.append(cp)

    def others(offsets):
        pairs = dict.fromkeys((a % weeks, b % regions) for a, b in offsets)
        return [p for p in pairs if p != (0, 0)]

    def signal(sem, offsets):
        for dw, dr in offsets:
            pl.semaphore_signal(sem, inc=1, device_id=there(dw, dr), device_id_type=MESH)

    w_off = week_offsets(weeks)
    near = others([(0, 1), (0, -1), (1, 1), (-1, -1), (1, 0), (-1, 0), (4, 0), (-4, 0)])
    rounds = [
        others([(4, 0), (-4, 0), (0, 1), (0, -1)]),
        others([(8, 0), (-8, 0), (0, 2), (0, -2)]),
        others([(1, 0), (-1, 0)]),
    ]
    barrier = pltpu.get_barrier_semaphore()
    signal(barrier, near)

    def spread(k):
        if k > 0 and rounds[k - 1]:
            pl.semaphore_wait(round_sem.at[k - 1], len(rounds[k - 1]))
        if k < len(rounds):
            signal(round_sem.at[k], rounds[k])

    def send(src, dst, ss, rs, to):
        pltpu.make_async_remote_copy(
            src_ref=src, dst_ref=dst, send_sem=ss, recv_sem=rs, device_id=to, device_id_type=MESH
        ).start()

    def wait_for(ref, sem):
        pltpu.make_async_copy(ref, ref, sem).wait()

    def span(c):
        return pl.ds(starts[c], sizes[c])

    def send_prices(y, yb, ss, rs, c):
        at = span(c)
        send(y.at[0:2, at], yb.at[3:5, at], ss, rs.at[c], there(-1, -1))
        send(y.at[0:1, at], yb.at[5:6, at], ss, rs.at[c], there(-1, 0))
        send(y.at[1:4, at], yb.at[0:3, at], ss, rs.at[c], there(0, -1))

    def send_arrivals(fs, fv, fb, ss, rs, c):
        at = span(c)
        send(fs.at[3:5, at], fb.at[3:5, at], ss, rs.at[c], there(1, 1))
        send(fv, fb.at[5:6, at], ss, rs.at[c], there(1, 0))
        send(fs.at[0:3, at], fb.at[0:3, at], ss, rs.at[c], there(0, 1))

    def mix(values, weight):
        hi = values.astype(BF16)
        lo = (values - hi.astype(F32)).astype(BF16)
        both = jnp.dot(jnp.concatenate([hi, lo], axis=1), weight[...], preferred_element_type=F32)
        return both[:, :PANEL] + both[:, PANEL:]

    def pulled_gradients(y, yb, c):
        pulled = mix(yb[0:5, span(c), :].reshape(5 * sizes[c], PANEL), w_adj)
        pulled = pulled.reshape(5, sizes[c], PANEL)
        pulled = [pulled[k] for k in range(5)]
        pulled[3] = jnp.where(last, 0.0, pulled[3])
        pulled[4] = jnp.where(last, 0.0, pulled[4])
        short = lead[span(c), :] == 1
        rows = [y[t, span(c), :] for t in range(ROWS)]
        after = rows[1:] + [jnp.where(last, 0.0, yb[5, span(c), :])]
        grad_v = [rows[t] - after[t] for t in range(ROWS)]
        grad_s = [rows[t] - jnp.where(short, pulled[t], pulled[t + 1]) for t in range(ROWS)]
        return grad_v, grad_s

    def mix_arrivals(rows, fs, c):
        short = lead[span(c), :] == 1
        lagged = jnp.concatenate(
            [
                jnp.where(short, rows[0], 0.0),
                jnp.where(short, rows[1], rows[0]),
                jnp.where(short, rows[2], rows[1]),
                jnp.where(short, rows[3], rows[2]),
                jnp.where(short, 0.0, rows[3]),
            ],
            axis=0,
        )
        fs[:, span(c), :] = mix(lagged, w_fwd).reshape(5, sizes[c], PANEL)

    def arrivals(fb, c):
        early = [jnp.where(first, 0.0, fb[3 + k, span(c), :]) for k in range(2)]
        own = [fb[k, span(c), :] for k in range(3)]
        return early, [early[0], own[0] + early[1], own[1], own[2]]

    def balance_of(v_rows, s_rows, fb, receipts, c):
        before = [jnp.where(first, 0.0, fb[5, span(c), :])] + v_rows[:-1]
        return [v_rows[t] - before[t] + s_rows[t] - receipts[t] for t in range(ROWS)]

    def fold(values):
        return jnp.sum(values.reshape(values.shape[0] // 8, 8, PANEL), axis=0)

    loads[0].wait()
    pl.semaphore_wait(barrier, len(near))
    for c in range(CHUNKS):
        send_prices(y0, yb0, send_sem.at[1], y0_rs, c)
    spread(0)

    loads[1].wait()
    for weight, dest in ((mixw[...], w_fwd), (mixw[...].T, w_adj)):
        hi = weight.astype(BF16)
        lo = (weight - hi.astype(F32)).astype(BF16)
        half = jnp.concatenate([hi, lo], axis=1)
        dest[...] = jnp.concatenate([half, half], axis=0)
    for cp in loads[2:5]:
        cp.wait()

    def send_start(c):
        send_arrivals(fs_1, v0.at[3:4, span(c)], fb_1, send_sem.at[0], f1_rs, c)

    for c in range(CHUNKS):
        mix_arrivals([s0[t, span(c), :] for t in range(ROWS)], fs_1, c)
        if c < CHUNKS // 2:
            send_start(c)
    for cp in loads[5:]:
        cp.wait()

    primal = jnp.zeros((8, PANEL), F32)
    dual = jnp.zeros((8, PANEL), F32)

    def first_primal(c, primal):
        wait_for(yb0.at[:, span(c)], y0_rs.at[c])
        grad_v, grad_s = pulled_gradients(y0, yb0, c)
        ahead = []
        for t in range(ROWS):
            old_v = v0[t, span(c), :]
            new_v = jnp.maximum(old_v - STEP_ETA * (ch[t, span(c), :] - grad_v[t]), 0.0)
            v1[t, span(c), :] = new_v
            if t == ROWS - 1:
                fv_t[0, span(c), :] = 2.0 * new_v - old_v
            old_s = s0[t, span(c), :]
            top = cap[t, span(c), :].astype(F32)
            new_s = jnp.minimum(
                jnp.maximum(old_s - STEP_ETA * (cs[t, span(c), :] - grad_s[t]), 0.0), top
            )
            s1[t, span(c), :] = new_s
            primal = primal + fold((new_v - old_v) ** 2) + fold((new_s - old_s) ** 2)
            ahead.append(2.0 * new_s - old_s)
        mix_arrivals(ahead, fs_t, c)
        send_arrivals(fs_t, fv_t.at[:, span(c)], fb_t, send_sem.at[2], ft_rs, c)
        return primal

    def first_dual(c, dual):
        wait_for(fb_t.at[:, span(c)], ft_rs.at[c])
        _, receipts = arrivals(fb_t, c)
        v_rows = [2.0 * v1[t, span(c), :] - v0[t, span(c), :] for t in range(ROWS)]
        s_rows = [2.0 * s1[t, span(c), :] - s0[t, span(c), :] for t in range(ROWS)]
        ahead = balance_of(v_rows, s_rows, fb_t, receipts, c)
        for t in range(ROWS):
            bal1[t, span(c), :] = ahead[t]
            moved = STEP_ETA * (dem[t, span(c), :] - ahead[t])
            new_y = y0[t, span(c), :] + moved
            y1[t, span(c), :] = new_y
            dual = dual + fold((new_y - y0[t, span(c), :]) ** 2)
        if c < CHUNKS - 1:
            send_prices(y1, yb1, send_sem.at[3], y1_rs, c)
        return dual

    for c in range(CHUNKS + LAG):
        if c < CHUNKS:
            primal = first_primal(c, primal)
        if c == CHUNKS - 1:
            for k in range(CHUNKS // 2, CHUNKS):
                send_start(k)
        if c >= LAG:
            dual = first_dual(c - LAG, dual)
        if 0 < c <= len(rounds):
            spread(c)

    lane = lax.broadcasted_iota(jnp.int32, (1, PANEL), 1)
    primal = jnp.sum(primal, axis=0, keepdims=True)
    dual = jnp.sum(dual, axis=0, keepdims=True)
    half = PANEL // 2
    mine = jnp.where(
        lane < half, primal + pltpu.roll(primal, half, 1), dual + pltpu.roll(dual, half, 1)
    )
    row1[...] = mine
    for d in w_off:
        send(row1, rows1.at[w], wide_sem.at[0], wide_sem.at[1], there(d, 0))
    rows1[w] = mine
    send_prices(y1, yb1, send_sem.at[3], y1_rs, CHUNKS - 1)

    wait_for(rows1.at[0 : weeks - 1], wide_sem.at[1])
    mine = jnp.sum(rows1[...], axis=0)
    row2[...] = mine
    for d in range(1, regions):
        send(row2, rows2.at[r], wide_sem.at[2], wide_sem.at[3], there(0, d))
    rows2[r] = mine

    for c in range(CHUNKS):
        wait_for(yb1.at[:, span(c)], y1_rs.at[c])
        grad_v, grad_s = pulled_gradients(y1, yb1, c)
        for t in range(ROWS):
            ch[t, span(c), :] = ch[t, span(c), :] - grad_v[t]
            cs[t, span(c), :] = cs[t, span(c), :] - grad_s[t]

    s_sum[...] = dem[0] + dem[1] + dem[2] + dem[3]

    wait_for(rows2.at[0 : regions - 1], wide_sem.at[3])
    total = jnp.sum(rows2[...], axis=0)
    moved_primal = jnp.sum(jnp.where(lane < half, total, 0.0), axis=1, keepdims=True)
    moved_dual = jnp.sum(jnp.where(lane < half, 0.0, total), axis=1, keepdims=True)
    ratio = jnp.broadcast_to((moved_dual + EPS_MOVE) / (moved_primal + EPS_MOVE), (1, PANEL))
    weight = jnp.sqrt(jnp.sqrt(ratio))
    primal_step = STEP_ETA / weight
    dual_step = STEP_ETA * weight

    owners = weeks // 4
    quarter = panels // 4

    def quarter_at(k):
        q = lax.rem(lax.div(w, owners) + k, 4)
        return q, pl.ds(pl.multiple_of(q * quarter, 8), quarter)

    for k in QUARTERS:
        _, at = quarter_at(k)
        sums = jnp.zeros((quarter, PANEL), F32)
        for t in range(ROWS):
            new_s = jnp.minimum(
                jnp.maximum(s1[t, at, :] - primal_step * cs[t, at, :], 0.0), cap[t, at, :].astype(F32)
            )
            s2[t, at, :] = new_s
            sums = sums + new_s
        s_sum[at, :] = s_sum[at, :] + sums
        m_send[at, :] = mix(sums, w_fwd)
        send(m_send.at[at], m_recv.at[at], wide_sem.at[4], m_rs.at[k], there(0, 1))

    def last_arrivals(c):
        for t in range(ROWS):
            v2[t, span(c), :] = jnp.maximum(v1[t, span(c), :] - primal_step * ch[t, span(c), :], 0.0)
        mix_arrivals([s2[t, span(c), :] for t in range(ROWS)], fs_2, c)
        send_arrivals(fs_2, v2.at[3:4, span(c)], fb_2, send_sem.at[4], f2_rs, c)

    for c in range(EARLY):
        last_arrivals(c)

    for k in QUARTERS:
        q, at = quarter_at(k)
        wait_for(m_recv.at[at], m_rs.at[k])
        net[at, :] = m_recv[at, :] - s_sum[at, :]
        for j in range(0 if k else 1, owners):
            to = q * owners + lax.rem(w + j, owners)
            send(net.at[pl.ds(to * piece, piece)], a1.at[w], wide_sem.at[5], wide_sem.at[6], (to, r))
    a1[w] = net[pl.ds(w * piece, piece), :]

    for c in range(EARLY, CHUNKS):
        last_arrivals(c)

    for c in range(CHUNKS):
        wait_for(fb_1.at[:, span(c)], f1_rs.at[c])
        _, receipts = arrivals(fb_1, c)
        v_rows = [v0[t, span(c), :] for t in range(ROWS)]
        s_rows = [s0[t, span(c), :] for t in range(ROWS)]
        rows = balance_of(v_rows, s_rows, fb_1, receipts, c)
        for t in range(ROWS):
            bal1[t, span(c), :] = 0.5 * (bal1[t, span(c), :] + rows[t])

    wait_for(a1.at[0 : weeks - 1], wide_sem.at[6])
    running = jnp.zeros((piece, PANEL), F32)
    for k in range(weeks):
        a2[k] = running
        running = running + a1[k]
    for d in w_off:
        to = there(d, 0)
        send(a2.at[to[0]], pref.at[pl.ds(w * piece, piece)], wide_sem.at[7], wide_sem.at[8], to)
    pref[pl.ds(w * piece, piece), :] = a2[w]

    for c in range(CHUNKS):
        wait_for(fb_2.at[:, span(c)], f2_rs.at[c])
        early, receipts = arrivals(fb_2, c)
        v_rows = [v2[t, span(c), :] for t in range(ROWS)]
        s_rows = [s2[t, span(c), :] for t in range(ROWS)]
        rows = balance_of(v_rows, s_rows, fb_2, receipts, c)
        flow = -early[0] - early[1]
        for t in range(ROWS):
            wanted = dem[t, span(c), :]
            y2[t, span(c), :] = y1[t, span(c), :] + dual_step * (
                wanted - 2.0 * rows[t] + bal1[t, span(c), :]
            )
            flow = flow + (receipts[t] - s_rows[t] - wanted)
            pj[t, span(c), :] = flow
    for k, landing in enumerate((fb_1, yb0, fb_t, yb1, fb_2)):
        wait_for(landing, send_sem.at[k])
    wait_for(rows1.at[0 : weeks - 1], wide_sem.at[0])
    wait_for(rows2.at[0 : regions - 1], wide_sem.at[2])
    wait_for(m_recv, wide_sem.at[4])
    wait_for(a1.at[0 : weeks - 1], wide_sem.at[5])
    wait_for(a2.at[0 : weeks - 1], wide_sem.at[7])
    wait_for(pref.at[0 : panels - piece], wide_sem.at[8])


def finish(v2, s2, y2, pj, pref, stock_out, ship_out, dual_out, proj_out, total, sem):
    copies = []
    for k, (src, dst) in enumerate(((v2, stock_out), (s2, ship_out), (y2, dual_out))):
        copies.append(pltpu.make_async_copy(src, dst, sem.at[k]))
        copies[-1].start()
    for t in range(ROWS):
        total[t] = pj[t] + pref[...]
        copies.append(pltpu.make_async_copy(total.at[t], proj_out.at[t], sem.at[3 + t]))
        copies[-1].start()
    for cp in copies:
        cp.wait()


def shards(weeks, regions, stock, ship, dual, demand, hold, cost, cap, lead, mix):
    items = stock.shape[-1]
    panels = items // PANEL

    def in_hbm(a, *shape):
        return pltpu.with_memory_space_constraint(a.reshape(shape), pltpu.HBM)

    def view(a):
        return in_hbm(a, ROWS, panels, PANEL)

    slab = (ROWS, panels, PANEL)

    def vmem(*shape, dtype=F32):
        return pltpu.VMEM(shape, dtype)

    def sems(n):
        return pltpu.SemaphoreType.DMA((n,))

    scratch = (
        [vmem(*slab)] * 6
        + [vmem(*slab, dtype=jnp.int32), vmem(panels, PANEL, dtype=jnp.int32), vmem(PANEL, PANEL)]
        + [vmem(2 * PANEL, 2 * PANEL, dtype=BF16)] * 2
        + [vmem(*slab)] * 4
        + [vmem(6, panels, PANEL)] * 2
        + [vmem(5, panels, PANEL), vmem(1, panels, PANEL), vmem(6, panels, PANEL)]
        + [vmem(5, panels, PANEL), vmem(6, panels, PANEL)] * 2
        + [vmem(panels, PANEL)] * 4
        + [vmem(weeks, panels // weeks, PANEL)] * 2
        + [vmem(1, PANEL), vmem(weeks, 1, PANEL), vmem(1, PANEL), vmem(regions, 1, PANEL)]
        + [sems(9), sems(5), sems(9), pltpu.SemaphoreType.REGULAR((3,))]
        + [sems(CHUNKS)] * 5
        + [sems(4)]
    )
    parts = pl.pallas_call(
        functools.partial(kernel, weeks, regions, panels),
        out_shape=[jax.ShapeDtypeStruct(slab, F32)] * 4
        + [jax.ShapeDtypeStruct((panels, PANEL), F32)],
        in_specs=[pl.BlockSpec(memory_space=pltpu.HBM)] * 9,
        out_specs=[pl.BlockSpec(memory_space=pltpu.VMEM)] * 5,
        scratch_shapes=scratch,
        compiler_params=pltpu.CompilerParams(
            collective_id=0, has_side_effects=True, vmem_limit_bytes=40 * 1024 * 1024
        ),
        cost_estimate=pl.CostEstimate(
            flops=2 * 6 * 5 * 5 * panels * PANEL * PANEL,
            bytes_accessed=12 * 4 * ROWS * panels * PANEL,
            transcendentals=0,
        ),
        name="primal_dual",
    )(
        view(stock), view(ship), view(dual), view(demand), view(hold), view(cost), view(cap),
        in_hbm(lead, panels, PANEL), in_hbm(mix, PANEL, PANEL),
    )
    outs = pl.pallas_call(
        finish,
        out_shape=[jax.ShapeDtypeStruct(slab, F32)] * 4,
        in_specs=[pl.BlockSpec(memory_space=pltpu.VMEM)] * 5,
        out_specs=[pl.BlockSpec(memory_space=pltpu.HBM)] * 4,
        scratch_shapes=[vmem(*slab), pltpu.SemaphoreType.DMA((3 + ROWS,))],
        compiler_params=pltpu.CompilerParams(vmem_limit_bytes=8 * 1024 * 1024),
        name="finish",
    )(*parts)
    return tuple(o.reshape(ROWS, 1, items) for o in outs)


def solution(mesh):
    block = P("week", "region", None)
    in_specs = (block,) * 7 + (P("region", None), P("region", None, None))
    body = functools.partial(shards, mesh.shape["week"], mesh.shape["region"])
    return jax.shard_map(
        body, mesh=mesh, in_specs=in_specs, out_specs=(block,) * 4, check_vma=False
    )
```

```python
import functools

import jax
import jax.numpy as jnp
from jax import lax
from jax.experimental import pallas as pl
from jax.experimental.pallas import tpu as pltpu
from jax.sharding import PartitionSpec as P

PANEL = 128
ROWS = 4
SHARES = (8, 8, 7, 6, 3)
CHUNKS = len(SHARES)
EARLY = 1
LATE = 2
QUARTERS = (2, 1, 3, 0)
LAG = 3
STEP_ETA = 0.25
EPS_MOVE = 1e-06
MESH = pl.DeviceIdType.MESH
F32 = jnp.float32
BF16 = jnp.bfloat16


def ring_distance(d, n):
    return min(d % n, -d % n)


def week_offsets(weeks):
    def hops(d):
        return ring_distance(d // 4, max(weeks // 4, 1)) + ring_distance(d % 4, 4)

    return sorted(range(1, weeks), key=lambda d: (-hops(d), d))


def kernel(weeks, regions, panels, *refs):
    (
        stock_in, ship_in, dual_in, demand_in, hold_in, cost_in, cap_in, lead_in, mix_in,
        v2, s2, y2, pj, pref,
        v0, s0, y0, dem, ch, cs, cap, lead, mixw,
        w_fwd, w_adj,
        v1, s1, y1, bal1,
        yb0, yb1,
        fs_t, fv_t, fb_t,
        fs_1, fb_1,
        fs_2, fb_2,
        m_send, m_recv, s_sum, net, a1, a2,
        row1, rows1, row2, rows2,
        load_sem, send_sem, wide_sem, round_sem,
        y0_rs, y1_rs, ft_rs, f1_rs, f2_rs, m_rs,
    ) = refs
    w = lax.axis_index("week")
    r = lax.axis_index("region")
    first = w == 0
    last = w == weeks - 1
    sizes = [panels * k // sum(SHARES) for k in SHARES]
    starts = [sum(sizes[:c]) for c in range(CHUNKS)]
    piece = panels // weeks

    def there(dw, dr):
        return (lax.rem(w + dw + weeks, weeks), lax.rem(r + dr + regions, regions))

    loads = []
    for k, (src, dst) in enumerate(
        (
            (dual_in, y0), (mix_in, mixw), (lead_in, lead), (ship_in, s0), (stock_in, v0),
            (hold_in, ch), (cost_in, cs), (cap_in, cap), (demand_in, dem),
        )
    ):
        cp = pltpu.make_async_copy(src, dst, load_sem.at[k])
        cp.start()
        loads.append(cp)

    def others(offsets):
        pairs = dict.fromkeys((a % weeks, b % regions) for a, b in offsets)
        return [p for p in pairs if p != (0, 0)]

    def signal(sem, offsets):
        for dw, dr in offsets:
            pl.semaphore_signal(sem, inc=1, device_id=there(dw, dr), device_id_type=MESH)

    w_off = week_offsets(weeks)
    near = others([(0, 1), (0, -1), (1, 1), (-1, -1), (1, 0), (-1, 0), (4, 0), (-4, 0)])
    rounds = [
        others([(4, 0), (-4, 0), (0, 1), (0, -1)]),
        others([(8, 0), (-8, 0), (0, 2), (0, -2)]),
        others([(1, 0), (-1, 0)]),
    ]
    barrier = pltpu.get_barrier_semaphore()
    signal(barrier, near)

    def spread(k):
        if k > 0 and rounds[k - 1]:
            pl.semaphore_wait(round_sem.at[k - 1], len(rounds[k - 1]))
        if k < len(rounds):
            signal(round_sem.at[k], rounds[k])

    def send(src, dst, ss, rs, to):
        pltpu.make_async_remote_copy(
            src_ref=src, dst_ref=dst, send_sem=ss, recv_sem=rs, device_id=to, device_id_type=MESH
        ).start()

    def wait_for(ref, sem):
        pltpu.make_async_copy(ref, ref, sem).wait()

    def span(c):
        return pl.ds(starts[c], sizes[c])

    def send_prices(y, yb, ss, rs, c):
        at = span(c)
        send(y.at[0:2, at], yb.at[3:5, at], ss, rs.at[c], there(-1, -1))
        send(y.at[0:1, at], yb.at[5:6, at], ss, rs.at[c], there(-1, 0))
        send(y.at[1:4, at], yb.at[0:3, at], ss, rs.at[c], there(0, -1))

    def send_arrivals(fs, fv, fb, ss, rs, c):
        at = span(c)
        send(fs.at[3:5, at], fb.at[3:5, at], ss, rs.at[c], there(1, 1))
        send(fv, fb.at[5:6, at], ss, rs.at[c], there(1, 0))
        send(fs.at[0:3, at], fb.at[0:3, at], ss, rs.at[c], there(0, 1))

    def mix(values, weight):
        hi = values.astype(BF16)
        lo = (values - hi.astype(F32)).astype(BF16)
        both = jnp.dot(jnp.concatenate([hi, lo], axis=1), weight[...], preferred_element_type=F32)
        return both[:, :PANEL] + both[:, PANEL:]

    def pulled_gradients(y, yb, c):
        pulled = mix(yb[0:5, span(c), :].reshape(5 * sizes[c], PANEL), w_adj)
        pulled = pulled.reshape(5, sizes[c], PANEL)
        pulled = [pulled[k] for k in range(5)]
        pulled[3] = jnp.where(last, 0.0, pulled[3])
        pulled[4] = jnp.where(last, 0.0, pulled[4])
        short = lead[span(c), :] == 1
        rows = [y[t, span(c), :] for t in range(ROWS)]
        after = rows[1:] + [jnp.where(last, 0.0, yb[5, span(c), :])]
        grad_v = [rows[t] - after[t] for t in range(ROWS)]
        grad_s = [rows[t] - jnp.where(short, pulled[t], pulled[t + 1]) for t in range(ROWS)]
        return grad_v, grad_s

    def mix_arrivals(rows, fs, c):
        short = lead[span(c), :] == 1
        lagged = jnp.concatenate(
            [
                jnp.where(short, rows[0], 0.0),
                jnp.where(short, rows[1], rows[0]),
                jnp.where(short, rows[2], rows[1]),
                jnp.where(short, rows[3], rows[2]),
                jnp.where(short, 0.0, rows[3]),
            ],
            axis=0,
        )
        fs[:, span(c), :] = mix(lagged, w_fwd).reshape(5, sizes[c], PANEL)

    def arrivals(fb, c):
        early = [jnp.where(first, 0.0, fb[3 + k, span(c), :]) for k in range(2)]
        own = [fb[k, span(c), :] for k in range(3)]
        return early, [early[0], own[0] + early[1], own[1], own[2]]

    def balance_of(v_rows, s_rows, fb, receipts, c):
        before = [jnp.where(first, 0.0, fb[5, span(c), :])] + v_rows[:-1]
        return [v_rows[t] - before[t] + s_rows[t] - receipts[t] for t in range(ROWS)]

    def fold(values):
        return jnp.sum(values.reshape(values.shape[0] // 8, 8, PANEL), axis=0)

    loads[1].wait()
    for weight, dest in ((mixw[...], w_fwd), (mixw[...].T, w_adj)):
        hi = weight.astype(BF16)
        lo = (weight - hi.astype(F32)).astype(BF16)
        half = jnp.concatenate([hi, lo], axis=1)
        dest[...] = jnp.concatenate([half, half], axis=0)
    for cp in loads[2:5]:
        cp.wait()

    def send_start(c):
        send_arrivals(fs_1, v0.at[3:4, span(c)], fb_1, send_sem.at[0], f1_rs, c)

    for c in range(CHUNKS):
        mix_arrivals([s0[t, span(c), :] for t in range(ROWS)], fs_1, c)

    loads[0].wait()
    pl.semaphore_wait(barrier, len(near))
    for c in range(CHUNKS):
        send_prices(y0, yb0, send_sem.at[1], y0_rs, c)
    spread(0)

    for c in range(CHUNKS // 2):
        send_start(c)
    for cp in loads[5:]:
        cp.wait()

    primal = jnp.zeros((8, PANEL), F32)
    dual = jnp.zeros((8, PANEL), F32)

    def first_primal(c, primal):
        wait_for(yb0.at[:, span(c)], y0_rs.at[c])
        grad_v, grad_s = pulled_gradients(y0, yb0, c)
        ahead = []
        for t in range(ROWS):
            old_v = v0[t, span(c), :]
            new_v = jnp.maximum(old_v - STEP_ETA * (ch[t, span(c), :] - grad_v[t]), 0.0)
            v1[t, span(c), :] = new_v
            if t == ROWS - 1:
                fv_t[0, span(c), :] = 2.0 * new_v - old_v
            old_s = s0[t, span(c), :]
            top = cap[t, span(c), :].astype(F32)
            new_s = jnp.minimum(
                jnp.maximum(old_s - STEP_ETA * (cs[t, span(c), :] - grad_s[t]), 0.0), top
            )
            s1[t, span(c), :] = new_s
            primal = primal + fold((new_v - old_v) ** 2) + fold((new_s - old_s) ** 2)
            ahead.append(2.0 * new_s - old_s)
        mix_arrivals(ahead, fs_t, c)
        send_arrivals(fs_t, fv_t.at[:, span(c)], fb_t, send_sem.at[2], ft_rs, c)
        return primal

    def first_dual(c, dual):
        wait_for(fb_t.at[:, span(c)], ft_rs.at[c])
        _, receipts = arrivals(fb_t, c)
        v_rows = [2.0 * v1[t, span(c), :] - v0[t, span(c), :] for t in range(ROWS)]
        s_rows = [2.0 * s1[t, span(c), :] - s0[t, span(c), :] for t in range(ROWS)]
        ahead = balance_of(v_rows, s_rows, fb_t, receipts, c)
        for t in range(ROWS):
            bal1[t, span(c), :] = ahead[t]
            moved = STEP_ETA * (dem[t, span(c), :] - ahead[t])
            new_y = y0[t, span(c), :] + moved
            y1[t, span(c), :] = new_y
            dual = dual + fold((new_y - y0[t, span(c), :]) ** 2)
        if c < CHUNKS - 1:
            send_prices(y1, yb1, send_sem.at[3], y1_rs, c)
        return dual

    for c in range(CHUNKS + LAG):
        if c < CHUNKS:
            primal = first_primal(c, primal)
        if c == CHUNKS - 1:
            for k in range(CHUNKS // 2, CHUNKS):
                send_start(k)
        if c >= LAG:
            dual = first_dual(c - LAG, dual)
        if 0 < c <= len(rounds):
            spread(c)

    lane = lax.broadcasted_iota(jnp.int32, (1, PANEL), 1)
    primal = jnp.sum(primal, axis=0, keepdims=True)
    dual = jnp.sum(dual, axis=0, keepdims=True)
    half = PANEL // 2
    mine = jnp.where(
        lane < half, primal + pltpu.roll(primal, half, 1), dual + pltpu.roll(dual, half, 1)
    )
    row1[...] = mine
    for d in w_off:
        send(row1, rows1.at[w], wide_sem.at[0], wide_sem.at[1], there(d, 0))
    rows1[w] = mine
    send_prices(y1, yb1, send_sem.at[3], y1_rs, CHUNKS - 1)

    wait_for(rows1.at[0 : weeks - 1], wide_sem.at[1])
    mine = jnp.sum(rows1[...], axis=0)
    row2[...] = mine
    for d in range(1, regions):
        send(row2, rows2.at[r], wide_sem.at[2], wide_sem.at[3], there(0, d))
    rows2[r] = mine

    for c in range(CHUNKS):
        wait_for(yb1.at[:, span(c)], y1_rs.at[c])
        grad_v, grad_s = pulled_gradients(y1, yb1, c)
        for t in range(ROWS):
            ch[t, span(c), :] = ch[t, span(c), :] - grad_v[t]
            cs[t, span(c), :] = cs[t, span(c), :] - grad_s[t]

    s_sum[...] = dem[0] + dem[1] + dem[2] + dem[3]

    wait_for(rows2.at[0 : regions - 1], wide_sem.at[3])
    total = jnp.sum(rows2[...], axis=0)
    moved_primal = jnp.sum(jnp.where(lane < half, total, 0.0), axis=1, keepdims=True)
    moved_dual = jnp.sum(jnp.where(lane < half, 0.0, total), axis=1, keepdims=True)
    ratio = jnp.broadcast_to((moved_dual + EPS_MOVE) / (moved_primal + EPS_MOVE), (1, PANEL))
    weight = jnp.sqrt(jnp.sqrt(ratio))
    primal_step = STEP_ETA / weight
    dual_step = STEP_ETA * weight

    owners = weeks // 4
    quarter = panels // 4

    def quarter_at(k):
        q = lax.rem(lax.div(w, owners) + k, 4)
        return q, pl.ds(pl.multiple_of(q * quarter, 8), quarter)

    for k in QUARTERS:
        _, at = quarter_at(k)
        sums = jnp.zeros((quarter, PANEL), F32)
        for t in range(ROWS):
            new_s = jnp.minimum(
                jnp.maximum(s1[t, at, :] - primal_step * cs[t, at, :], 0.0), cap[t, at, :].astype(F32)
            )
            s2[t, at, :] = new_s
            sums = sums + new_s
        s_sum[at, :] = s_sum[at, :] + sums
        m_send[at, :] = mix(sums, w_fwd)
        send(m_send.at[at], m_recv.at[at], wide_sem.at[4], m_rs.at[k], there(0, 1))

    def last_arrivals(c):
        for t in range(ROWS):
            v2[t, span(c), :] = jnp.maximum(v1[t, span(c), :] - primal_step * ch[t, span(c), :], 0.0)
        mix_arrivals([s2[t, span(c), :] for t in range(ROWS)], fs_2, c)
        send_arrivals(fs_2, v2.at[3:4, span(c)], fb_2, send_sem.at[4], f2_rs, c)

    for c in range(EARLY):
        last_arrivals(c)

    for k in QUARTERS:
        q, at = quarter_at(k)
        wait_for(m_recv.at[at], m_rs.at[k])
        net[at, :] = m_recv[at, :] - s_sum[at, :]
        for j in range(0 if k else 1, owners):
            to = q * owners + lax.rem(w + j, owners)
            send(net.at[pl.ds(to * piece, piece)], a1.at[w], wide_sem.at[5], wide_sem.at[6], (to, r))
    a1[w] = net[pl.ds(w * piece, piece), :]

    for c in range(EARLY, CHUNKS - LATE):
        last_arrivals(c)

    for c in range(CHUNKS):
        wait_for(fb_1.at[:, span(c)], f1_rs.at[c])
        _, receipts = arrivals(fb_1, c)
        v_rows = [v0[t, span(c), :] for t in range(ROWS)]
        s_rows = [s0[t, span(c), :] for t in range(ROWS)]
        rows = balance_of(v_rows, s_rows, fb_1, receipts, c)
        for t in range(ROWS):
            bal1[t, span(c), :] = 0.5 * (bal1[t, span(c), :] + rows[t])

    wait_for(a1.at[0 : weeks - 1], wide_sem.at[6])
    running = jnp.zeros((piece, PANEL), F32)
    for k in range(weeks):
        a2[k] = running
        running = running + a1[k]
    for d in w_off:
        to = there(d, 0)
        send(a2.at[to[0]], pref.at[pl.ds(w * piece, piece)], wide_sem.at[7], wide_sem.at[8], to)
    pref[pl.ds(w * piece, piece), :] = a2[w]

    for c in range(CHUNKS - LATE, CHUNKS):
        last_arrivals(c)

    for c in range(CHUNKS):
        wait_for(fb_2.at[:, span(c)], f2_rs.at[c])
        early, receipts = arrivals(fb_2, c)
        v_rows = [v2[t, span(c), :] for t in range(ROWS)]
        s_rows = [s2[t, span(c), :] for t in range(ROWS)]
        rows = balance_of(v_rows, s_rows, fb_2, receipts, c)
        flow = -early[0] - early[1]
        for t in range(ROWS):
            wanted = dem[t, span(c), :]
            y2[t, span(c), :] = y1[t, span(c), :] + dual_step * (
                wanted - 2.0 * rows[t] + bal1[t, span(c), :]
            )
            flow = flow + (receipts[t] - s_rows[t] - wanted)
            pj[t, span(c), :] = flow
    for k, landing in enumerate((fb_1, yb0, fb_t, yb1, fb_2)):
        wait_for(landing, send_sem.at[k])
    wait_for(rows1.at[0 : weeks - 1], wide_sem.at[0])
    wait_for(rows2.at[0 : regions - 1], wide_sem.at[2])
    wait_for(m_recv, wide_sem.at[4])
    wait_for(a1.at[0 : weeks - 1], wide_sem.at[5])
    wait_for(a2.at[0 : weeks - 1], wide_sem.at[7])
    wait_for(pref.at[0 : panels - piece], wide_sem.at[8])


def finish(v2, s2, y2, pj, pref, stock_out, ship_out, dual_out, proj_out, total, sem):
    copies = []
    for k, (src, dst) in enumerate(((v2, stock_out), (s2, ship_out), (y2, dual_out))):
        copies.append(pltpu.make_async_copy(src, dst, sem.at[k]))
        copies[-1].start()
    for t in range(ROWS):
        total[t] = pj[t] + pref[...]
        copies.append(pltpu.make_async_copy(total.at[t], proj_out.at[t], sem.at[3 + t]))
        copies[-1].start()
    for cp in copies:
        cp.wait()


def shards(weeks, regions, stock, ship, dual, demand, hold, cost, cap, lead, mix):
    items = stock.shape[-1]
    panels = items // PANEL

    def in_hbm(a, *shape):
        return pltpu.with_memory_space_constraint(a.reshape(shape), pltpu.HBM)

    def view(a):
        return in_hbm(a, ROWS, panels, PANEL)

    slab = (ROWS, panels, PANEL)

    def vmem(*shape, dtype=F32):
        return pltpu.VMEM(shape, dtype)

    def sems(n):
        return pltpu.SemaphoreType.DMA((n,))

    scratch = (
        [vmem(*slab)] * 6
        + [vmem(*slab, dtype=jnp.int32), vmem(panels, PANEL, dtype=jnp.int32), vmem(PANEL, PANEL)]
        + [vmem(2 * PANEL, 2 * PANEL, dtype=BF16)] * 2
        + [vmem(*slab)] * 4
        + [vmem(6, panels, PANEL)] * 2
        + [vmem(5, panels, PANEL), vmem(1, panels, PANEL), vmem(6, panels, PANEL)]
        + [vmem(5, panels, PANEL), vmem(6, panels, PANEL)] * 2
        + [vmem(panels, PANEL)] * 4
        + [vmem(weeks, panels // weeks, PANEL)] * 2
        + [vmem(1, PANEL), vmem(weeks, 1, PANEL), vmem(1, PANEL), vmem(regions, 1, PANEL)]
        + [sems(9), sems(5), sems(9), pltpu.SemaphoreType.REGULAR((3,))]
        + [sems(CHUNKS)] * 5
        + [sems(4)]
    )
    parts = pl.pallas_call(
        functools.partial(kernel, weeks, regions, panels),
        out_shape=[jax.ShapeDtypeStruct(slab, F32)] * 4
        + [jax.ShapeDtypeStruct((panels, PANEL), F32)],
        in_specs=[pl.BlockSpec(memory_space=pltpu.HBM)] * 9,
        out_specs=[pl.BlockSpec(memory_space=pltpu.VMEM)] * 5,
        scratch_shapes=scratch,
        compiler_params=pltpu.CompilerParams(
            collective_id=0, has_side_effects=True, vmem_limit_bytes=40 * 1024 * 1024
        ),
        cost_estimate=pl.CostEstimate(
            flops=2 * 6 * 5 * 5 * panels * PANEL * PANEL,
            bytes_accessed=12 * 4 * ROWS * panels * PANEL,
            transcendentals=0,
        ),
        name="primal_dual",
    )(
        view(stock), view(ship), view(dual), view(demand), view(hold), view(cost), view(cap),
        in_hbm(lead, panels, PANEL), in_hbm(mix, PANEL, PANEL),
    )
    outs = pl.pallas_call(
        finish,
        out_shape=[jax.ShapeDtypeStruct(slab, F32)] * 4,
        in_specs=[pl.BlockSpec(memory_space=pltpu.VMEM)] * 5,
        out_specs=[pl.BlockSpec(memory_space=pltpu.HBM)] * 4,
        scratch_shapes=[vmem(*slab), pltpu.SemaphoreType.DMA((3 + ROWS,))],
        compiler_params=pltpu.CompilerParams(vmem_limit_bytes=8 * 1024 * 1024),
        name="finish",
    )(*parts)
    return tuple(o.reshape(ROWS, 1, items) for o in outs)


def solution(mesh):
    block = P("week", "region", None)
    in_specs = (block,) * 7 + (P("region", None), P("region", None, None))
    body = functools.partial(shards, mesh.shape["week"], mesh.shape["region"])
    return jax.shard_map(
        body, mesh=mesh, in_specs=in_specs, out_specs=(block,) * 4, check_vma=False
    )
```

```python
import functools

import jax
import jax.numpy as jnp
from jax import lax
from jax.experimental import pallas as pl
from jax.experimental.pallas import tpu as pltpu
from jax.sharding import PartitionSpec as P

PANEL = 128
ROWS = 4
SHARES = (8, 8, 7, 6, 3)
CHUNKS = len(SHARES)
EARLY = 1
LATE = 1
QUARTERS = (2, 1, 3, 0)
LAG = 3
STEP_ETA = 0.25
EPS_MOVE = 1e-06
MESH = pl.DeviceIdType.MESH
F32 = jnp.float32
BF16 = jnp.bfloat16


def ring_distance(d, n):
    return min(d % n, -d % n)


def week_offsets(weeks):
    def hops(d):
        return ring_distance(d // 4, max(weeks // 4, 1)) + ring_distance(d % 4, 4)

    return sorted(range(1, weeks), key=lambda d: (-hops(d), d))


def kernel(weeks, regions, panels, *refs):
    (
        stock_in, ship_in, dual_in, demand_in, hold_in, cost_in, cap_in, lead_in, mix_in,
        v2, s2, y2, pj, pref,
        v0, s0, y0, dem, ch, cs, cap, lead, mixw,
        w_fwd, w_adj,
        v1, s1, y1, bal1,
        yb0, yb1,
        fs_t, fv_t, fb_t,
        fs_1, fb_1,
        fs_2, fb_2,
        m_send, m_recv, s_sum, net, a1, a2,
        row1, rows1, row2, rows2,
        load_sem, send_sem, wide_sem, round_sem,
        y0_rs, y1_rs, ft_rs, f1_rs, f2_rs, m_rs,
    ) = refs
    w = lax.axis_index("week")
    r = lax.axis_index("region")
    first = w == 0
    last = w == weeks - 1
    sizes = [panels * k // sum(SHARES) for k in SHARES]
    starts = [sum(sizes[:c]) for c in range(CHUNKS)]
    piece = panels // weeks

    def there(dw, dr):
        return (lax.rem(w + dw + weeks, weeks), lax.rem(r + dr + regions, regions))

    loads = []
    for k, (src, dst) in enumerate(
        (
            (dual_in, y0), (mix_in, mixw), (lead_in, lead), (ship_in, s0), (stock_in, v0),
            (hold_in, ch), (cost_in, cs), (cap_in, cap), (demand_in, dem),
        )
    ):
        cp = pltpu.make_async_copy(src, dst, load_sem.at[k])
        cp.start()
        loads.append(cp)

    def others(offsets):
        pairs = dict.fromkeys((a % weeks, b % regions) for a, b in offsets)
        return [p for p in pairs if p != (0, 0)]

    def signal(sem, offsets):
        for dw, dr in offsets:
            pl.semaphore_signal(sem, inc=1, device_id=there(dw, dr), device_id_type=MESH)

    w_off = week_offsets(weeks)
    near = others([(0, 1), (0, -1), (1, 1), (-1, -1), (1, 0), (-1, 0), (4, 0), (-4, 0)])
    rounds = [
        others([(4, 0), (-4, 0), (0, 1), (0, -1)]),
        others([(8, 0), (-8, 0), (0, 2), (0, -2)]),
        others([(1, 0), (-1, 0)]),
    ]
    barrier = pltpu.get_barrier_semaphore()
    signal(barrier, near)

    def spread(k):
        if k > 0 and rounds[k - 1]:
            pl.semaphore_wait(round_sem.at[k - 1], len(rounds[k - 1]))
        if k < len(rounds):
            signal(round_sem.at[k], rounds[k])

    def send(src, dst, ss, rs, to):
        pltpu.make_async_remote_copy(
            src_ref=src, dst_ref=dst, send_sem=ss, recv_sem=rs, device_id=to, device_id_type=MESH
        ).start()

    def wait_for(ref, sem):
        pltpu.make_async_copy(ref, ref, sem).wait()

    def span(c):
        return pl.ds(starts[c], sizes[c])

    def send_prices(y, yb, ss, rs, c):
        at = span(c)
        send(y.at[0:2, at], yb.at[3:5, at], ss, rs.at[c], there(-1, -1))
        send(y.at[0:1, at], yb.at[5:6, at], ss, rs.at[c], there(-1, 0))
        send(y.at[1:4, at], yb.at[0:3, at], ss, rs.at[c], there(0, -1))

    def send_arrivals(fs, fv, fb, ss, rs, c):
        at = span(c)
        send(fs.at[3:5, at], fb.at[3:5, at], ss, rs.at[c], there(1, 1))
        send(fv, fb.at[5:6, at], ss, rs.at[c], there(1, 0))
        send(fs.at[0:3, at], fb.at[0:3, at], ss, rs.at[c], there(0, 1))

    def mix(values, weight):
        hi = values.astype(BF16)
        lo = (values - hi.astype(F32)).astype(BF16)
        both = jnp.dot(jnp.concatenate([hi, lo], axis=1), weight[...], preferred_element_type=F32)
        return both[:, :PANEL] + both[:, PANEL:]

    def pulled_gradients(y, yb, c):
        pulled = mix(yb[0:5, span(c), :].reshape(5 * sizes[c], PANEL), w_adj)
        pulled = pulled.reshape(5, sizes[c], PANEL)
        pulled = [pulled[k] for k in range(5)]
        pulled[3] = jnp.where(last, 0.0, pulled[3])
        pulled[4] = jnp.where(last, 0.0, pulled[4])
        short = lead[span(c), :] == 1
        rows = [y[t, span(c), :] for t in range(ROWS)]
        after = rows[1:] + [jnp.where(last, 0.0, yb[5, span(c), :])]
        grad_v = [rows[t] - after[t] for t in range(ROWS)]
        grad_s = [rows[t] - jnp.where(short, pulled[t], pulled[t + 1]) for t in range(ROWS)]
        return grad_v, grad_s

    def mix_arrivals(rows, fs, c):
        short = lead[span(c), :] == 1
        lagged = jnp.concatenate(
            [
                jnp.where(short, rows[0], 0.0),
                jnp.where(short, rows[1], rows[0]),
                jnp.where(short, rows[2], rows[1]),
                jnp.where(short, rows[3], rows[2]),
                jnp.where(short, 0.0, rows[3]),
            ],
            axis=0,
        )
        fs[:, span(c), :] = mix(lagged, w_fwd).reshape(5, sizes[c], PANEL)

    def arrivals(fb, c):
        early = [jnp.where(first, 0.0, fb[3 + k, span(c), :]) for k in range(2)]
        own = [fb[k, span(c), :] for k in range(3)]
        return early, [early[0], own[0] + early[1], own[1], own[2]]

    def balance_of(v_rows, s_rows, fb, receipts, c):
        before = [jnp.where(first, 0.0, fb[5, span(c), :])] + v_rows[:-1]
        return [v_rows[t] - before[t] + s_rows[t] - receipts[t] for t in range(ROWS)]

    def fold(values):
        return jnp.sum(values.reshape(values.shape[0] // 8, 8, PANEL), axis=0)

    loads[1].wait()
    for weight, dest in ((mixw[...], w_fwd), (mixw[...].T, w_adj)):
        hi = weight.astype(BF16)
        lo = (weight - hi.astype(F32)).astype(BF16)
        half = jnp.concatenate([hi, lo], axis=1)
        dest[...] = jnp.concatenate([half, half], axis=0)
    for cp in loads[2:5]:
        cp.wait()

    def send_start(c):
        send_arrivals(fs_1, v0.at[3:4, span(c)], fb_1, send_sem.at[0], f1_rs, c)

    for c in range(CHUNKS):
        mix_arrivals([s0[t, span(c), :] for t in range(ROWS)], fs_1, c)

    loads[0].wait()
    pl.semaphore_wait(barrier, len(near))
    for c in range(CHUNKS):
        send_prices(y0, yb0, send_sem.at[1], y0_rs, c)
    spread(0)

    for c in range(CHUNKS // 2):
        send_start(c)
    for cp in loads[5:]:
        cp.wait()

    primal = jnp.zeros((8, PANEL), F32)
    dual = jnp.zeros((8, PANEL), F32)

    def first_primal(c, primal):
        wait_for(yb0.at[:, span(c)], y0_rs.at[c])
        grad_v, grad_s = pulled_gradients(y0, yb0, c)
        ahead = []
        for t in range(ROWS):
            old_v = v0[t, span(c), :]
            new_v = jnp.maximum(old_v - STEP_ETA * (ch[t, span(c), :] - grad_v[t]), 0.0)
            v1[t, span(c), :] = new_v
            if t == ROWS - 1:
                fv_t[0, span(c), :] = 2.0 * new_v - old_v
            old_s = s0[t, span(c), :]
            top = cap[t, span(c), :].astype(F32)
            new_s = jnp.minimum(
                jnp.maximum(old_s - STEP_ETA * (cs[t, span(c), :] - grad_s[t]), 0.0), top
            )
            s1[t, span(c), :] = new_s
            primal = primal + fold((new_v - old_v) ** 2) + fold((new_s - old_s) ** 2)
            ahead.append(2.0 * new_s - old_s)
        mix_arrivals(ahead, fs_t, c)
        send_arrivals(fs_t, fv_t.at[:, span(c)], fb_t, send_sem.at[2], ft_rs, c)
        return primal

    def first_dual(c, dual):
        wait_for(fb_t.at[:, span(c)], ft_rs.at[c])
        _, receipts = arrivals(fb_t, c)
        v_rows = [2.0 * v1[t, span(c), :] - v0[t, span(c), :] for t in range(ROWS)]
        s_rows = [2.0 * s1[t, span(c), :] - s0[t, span(c), :] for t in range(ROWS)]
        ahead = balance_of(v_rows, s_rows, fb_t, receipts, c)
        for t in range(ROWS):
            bal1[t, span(c), :] = ahead[t]
            moved = STEP_ETA * (dem[t, span(c), :] - ahead[t])
            new_y = y0[t, span(c), :] + moved
            y1[t, span(c), :] = new_y
            dual = dual + fold((new_y - y0[t, span(c), :]) ** 2)
        if c < CHUNKS - 1:
            send_prices(y1, yb1, send_sem.at[3], y1_rs, c)
        return dual

    for c in range(CHUNKS + LAG):
        if c < CHUNKS:
            primal = first_primal(c, primal)
        if c == CHUNKS - 1:
            for k in range(CHUNKS // 2, CHUNKS):
                send_start(k)
        if c >= LAG:
            dual = first_dual(c - LAG, dual)
        if 0 < c <= len(rounds):
            spread(c)

    lane = lax.broadcasted_iota(jnp.int32, (1, PANEL), 1)
    primal = jnp.sum(primal, axis=0, keepdims=True)
    dual = jnp.sum(dual, axis=0, keepdims=True)
    half = PANEL // 2
    mine = jnp.where(
        lane < half, primal + pltpu.roll(primal, half, 1), dual + pltpu.roll(dual, half, 1)
    )
    row1[...] = mine
    for d in w_off:
        send(row1, rows1.at[w], wide_sem.at[0], wide_sem.at[1], there(d, 0))
    rows1[w] = mine
    send_prices(y1, yb1, send_sem.at[3], y1_rs, CHUNKS - 1)

    wait_for(rows1.at[0 : weeks - 1], wide_sem.at[1])
    mine = jnp.sum(rows1[...], axis=0)
    row2[...] = mine
    for d in range(1, regions):
        send(row2, rows2.at[r], wide_sem.at[2], wide_sem.at[3], there(0, d))
    rows2[r] = mine

    for c in range(CHUNKS):
        wait_for(yb1.at[:, span(c)], y1_rs.at[c])
        grad_v, grad_s = pulled_gradients(y1, yb1, c)
        for t in range(ROWS):
            ch[t, span(c), :] = ch[t, span(c), :] - grad_v[t]
            cs[t, span(c), :] = cs[t, span(c), :] - grad_s[t]

    s_sum[...] = dem[0] + dem[1] + dem[2] + dem[3]

    wait_for(rows2.at[0 : regions - 1], wide_sem.at[3])
    total = jnp.sum(rows2[...], axis=0)
    moved_primal = jnp.sum(jnp.where(lane < half, total, 0.0), axis=1, keepdims=True)
    moved_dual = jnp.sum(jnp.where(lane < half, 0.0, total), axis=1, keepdims=True)
    ratio = jnp.broadcast_to((moved_dual + EPS_MOVE) / (moved_primal + EPS_MOVE), (1, PANEL))
    weight = jnp.sqrt(jnp.sqrt(ratio))
    primal_step = STEP_ETA / weight
    dual_step = STEP_ETA * weight

    owners = weeks // 4
    quarter = panels // 4

    def quarter_at(k):
        q = lax.rem(lax.div(w, owners) + k, 4)
        return q, pl.ds(pl.multiple_of(q * quarter, 8), quarter)

    for k in QUARTERS:
        _, at = quarter_at(k)
        sums = jnp.zeros((quarter, PANEL), F32)
        for t in range(ROWS):
            new_s = jnp.minimum(
                jnp.maximum(s1[t, at, :] - primal_step * cs[t, at, :], 0.0), cap[t, at, :].astype(F32)
            )
            s2[t, at, :] = new_s
            sums = sums + new_s
        s_sum[at, :] = s_sum[at, :] + sums
        m_send[at, :] = mix(sums, w_fwd)
        send(m_send.at[at], m_recv.at[at], wide_sem.at[4], m_rs.at[k], there(0, 1))

    def last_arrivals(c):
        for t in range(ROWS):
            v2[t, span(c), :] = jnp.maximum(v1[t, span(c), :] - primal_step * ch[t, span(c), :], 0.0)
        mix_arrivals([s2[t, span(c), :] for t in range(ROWS)], fs_2, c)
        send_arrivals(fs_2, v2.at[3:4, span(c)], fb_2, send_sem.at[4], f2_rs, c)

    for c in range(EARLY):
        last_arrivals(c)

    for k in QUARTERS:
        q, at = quarter_at(k)
        wait_for(m_recv.at[at], m_rs.at[k])
        net[at, :] = m_recv[at, :] - s_sum[at, :]
        for j in range(0 if k else 1, owners):
            to = q * owners + lax.rem(w + j, owners)
            send(net.at[pl.ds(to * piece, piece)], a1.at[w], wide_sem.at[5], wide_sem.at[6], (to, r))
    a1[w] = net[pl.ds(w * piece, piece), :]

    for c in range(EARLY, CHUNKS - LATE):
        last_arrivals(c)

    for c in range(CHUNKS):
        wait_for(fb_1.at[:, span(c)], f1_rs.at[c])
        _, receipts = arrivals(fb_1, c)
        v_rows = [v0[t, span(c), :] for t in range(ROWS)]
        s_rows = [s0[t, span(c), :] for t in range(ROWS)]
        rows = balance_of(v_rows, s_rows, fb_1, receipts, c)
        for t in range(ROWS):
            bal1[t, span(c), :] = 0.5 * (bal1[t, span(c), :] + rows[t])

    wait_for(a1.at[0 : weeks - 1], wide_sem.at[6])
    running = jnp.zeros((piece, PANEL), F32)
    for k in range(weeks):
        a2[k] = running
        running = running + a1[k]
    for d in w_off:
        to = there(d, 0)
        send(a2.at[to[0]], pref.at[pl.ds(w * piece, piece)], wide_sem.at[7], wide_sem.at[8], to)
    pref[pl.ds(w * piece, piece), :] = a2[w]

    for c in range(CHUNKS - LATE, CHUNKS):
        last_arrivals(c)

    for c in range(CHUNKS):
        wait_for(fb_2.at[:, span(c)], f2_rs.at[c])
        early, receipts = arrivals(fb_2, c)
        v_rows = [v2[t, span(c), :] for t in range(ROWS)]
        s_rows = [s2[t, span(c), :] for t in range(ROWS)]
        rows = balance_of(v_rows, s_rows, fb_2, receipts, c)
        flow = -early[0] - early[1]
        for t in range(ROWS):
            wanted = dem[t, span(c), :]
            y2[t, span(c), :] = y1[t, span(c), :] + dual_step * (
                wanted - 2.0 * rows[t] + bal1[t, span(c), :]
            )
            flow = flow + (receipts[t] - s_rows[t] - wanted)
            pj[t, span(c), :] = flow
    for k, landing in enumerate((fb_1, yb0, fb_t, yb1, fb_2)):
        wait_for(landing, send_sem.at[k])
    wait_for(rows1.at[0 : weeks - 1], wide_sem.at[0])
    wait_for(rows2.at[0 : regions - 1], wide_sem.at[2])
    wait_for(m_recv, wide_sem.at[4])
    wait_for(a1.at[0 : weeks - 1], wide_sem.at[5])
    wait_for(a2.at[0 : weeks - 1], wide_sem.at[7])
    wait_for(pref.at[0 : panels - piece], wide_sem.at[8])


def finish(v2, s2, y2, pj, pref, stock_out, ship_out, dual_out, proj_out, total, sem):
    copies = []
    for k, (src, dst) in enumerate(((v2, stock_out), (s2, ship_out), (y2, dual_out))):
        copies.append(pltpu.make_async_copy(src, dst, sem.at[k]))
        copies[-1].start()
    for t in range(ROWS):
        total[t] = pj[t] + pref[...]
        copies.append(pltpu.make_async_copy(total.at[t], proj_out.at[t], sem.at[3 + t]))
        copies[-1].start()
    for cp in copies:
        cp.wait()


def shards(weeks, regions, stock, ship, dual, demand, hold, cost, cap, lead, mix):
    items = stock.shape[-1]
    panels = items // PANEL

    def in_hbm(a, *shape):
        return pltpu.with_memory_space_constraint(a.reshape(shape), pltpu.HBM)

    def view(a):
        return in_hbm(a, ROWS, panels, PANEL)

    slab = (ROWS, panels, PANEL)

    def vmem(*shape, dtype=F32):
        return pltpu.VMEM(shape, dtype)

    def sems(n):
        return pltpu.SemaphoreType.DMA((n,))

    scratch = (
        [vmem(*slab)] * 6
        + [vmem(*slab, dtype=jnp.int32), vmem(panels, PANEL, dtype=jnp.int32), vmem(PANEL, PANEL)]
        + [vmem(2 * PANEL, 2 * PANEL, dtype=BF16)] * 2
        + [vmem(*slab)] * 4
        + [vmem(6, panels, PANEL)] * 2
        + [vmem(5, panels, PANEL), vmem(1, panels, PANEL), vmem(6, panels, PANEL)]
        + [vmem(5, panels, PANEL), vmem(6, panels, PANEL)] * 2
        + [vmem(panels, PANEL)] * 4
        + [vmem(weeks, panels // weeks, PANEL)] * 2
        + [vmem(1, PANEL), vmem(weeks, 1, PANEL), vmem(1, PANEL), vmem(regions, 1, PANEL)]
        + [sems(9), sems(5), sems(9), pltpu.SemaphoreType.REGULAR((3,))]
        + [sems(CHUNKS)] * 5
        + [sems(4)]
    )
    parts = pl.pallas_call(
        functools.partial(kernel, weeks, regions, panels),
        out_shape=[jax.ShapeDtypeStruct(slab, F32)] * 4
        + [jax.ShapeDtypeStruct((panels, PANEL), F32)],
        in_specs=[pl.BlockSpec(memory_space=pltpu.HBM)] * 9,
        out_specs=[pl.BlockSpec(memory_space=pltpu.VMEM)] * 5,
        scratch_shapes=scratch,
        compiler_params=pltpu.CompilerParams(
            collective_id=0, has_side_effects=True, vmem_limit_bytes=40 * 1024 * 1024
        ),
        cost_estimate=pl.CostEstimate(
            flops=2 * 6 * 5 * 5 * panels * PANEL * PANEL,
            bytes_accessed=12 * 4 * ROWS * panels * PANEL,
            transcendentals=0,
        ),
        name="primal_dual",
    )(
        view(stock), view(ship), view(dual), view(demand), view(hold), view(cost), view(cap),
        in_hbm(lead, panels, PANEL), in_hbm(mix, PANEL, PANEL),
    )
    outs = pl.pallas_call(
        finish,
        out_shape=[jax.ShapeDtypeStruct(slab, F32)] * 4,
        in_specs=[pl.BlockSpec(memory_space=pltpu.VMEM)] * 5,
        out_specs=[pl.BlockSpec(memory_space=pltpu.HBM)] * 4,
        scratch_shapes=[vmem(*slab), pltpu.SemaphoreType.DMA((3 + ROWS,))],
        compiler_params=pltpu.CompilerParams(vmem_limit_bytes=8 * 1024 * 1024),
        name="finish",
    )(*parts)
    return tuple(o.reshape(ROWS, 1, items) for o in outs)


def solution(mesh):
    block = P("week", "region", None)
    in_specs = (block,) * 7 + (P("region", None), P("region", None, None))
    body = functools.partial(shards, mesh.shape["week"], mesh.shape["region"])
    return jax.shard_map(
        body, mesh=mesh, in_specs=in_specs, out_specs=(block,) * 4, check_vma=False
    )
```

```python
import functools

import jax
import jax.numpy as jnp
from jax import lax
from jax.experimental import pallas as pl
from jax.experimental.pallas import tpu as pltpu
from jax.sharding import PartitionSpec as P

PANEL = 128
ROWS = 4
SHARES = (10, 8, 7, 5, 2)
CHUNKS = len(SHARES)
EARLY = 1
LATE = 1
QUARTERS = (2, 1, 3, 0)
LAG = 3
STEP_ETA = 0.25
EPS_MOVE = 1e-06
MESH = pl.DeviceIdType.MESH
F32 = jnp.float32
BF16 = jnp.bfloat16


def ring_distance(d, n):
    return min(d % n, -d % n)


def week_offsets(weeks):
    def hops(d):
        return ring_distance(d // 4, max(weeks // 4, 1)) + ring_distance(d % 4, 4)

    return sorted(range(1, weeks), key=lambda d: (-hops(d), d))


def kernel(weeks, regions, panels, *refs):
    (
        stock_in, ship_in, dual_in, demand_in, hold_in, cost_in, cap_in, lead_in, mix_in,
        v2, s2, y2, pj, pref,
        v0, s0, y0, dem, ch, cs, cap, lead, mixw,
        w_fwd, w_adj,
        v1, s1, y1, bal1,
        yb0, yb1,
        fs_t, fv_t, fb_t,
        fs_1, fb_1,
        fs_2, fb_2,
        m_send, m_recv, s_sum, net, a1, a2,
        row1, rows1, row2, rows2,
        load_sem, send_sem, wide_sem, round_sem,
        y0_rs, y1_rs, ft_rs, f1_rs, f2_rs, m_rs,
    ) = refs
    w = lax.axis_index("week")
    r = lax.axis_index("region")
    first = w == 0
    last = w == weeks - 1
    sizes = [panels * k // sum(SHARES) for k in SHARES]
    starts = [sum(sizes[:c]) for c in range(CHUNKS)]
    piece = panels // weeks

    def there(dw, dr):
        return (lax.rem(w + dw + weeks, weeks), lax.rem(r + dr + regions, regions))

    loads = []
    for k, (src, dst) in enumerate(
        (
            (dual_in, y0), (mix_in, mixw), (lead_in, lead), (ship_in, s0), (stock_in, v0),
            (hold_in, ch), (cost_in, cs), (cap_in, cap), (demand_in, dem),
        )
    ):
        cp = pltpu.make_async_copy(src, dst, load_sem.at[k])
        cp.start()
        loads.append(cp)

    def others(offsets):
        pairs = dict.fromkeys((a % weeks, b % regions) for a, b in offsets)
        return [p for p in pairs if p != (0, 0)]

    def signal(sem, offsets):
        for dw, dr in offsets:
            pl.semaphore_signal(sem, inc=1, device_id=there(dw, dr), device_id_type=MESH)

    w_off = week_offsets(weeks)
    near = others([(0, 1), (0, -1), (1, 1), (-1, -1), (1, 0), (-1, 0), (4, 0), (-4, 0)])
    rounds = [
        others([(4, 0), (-4, 0), (0, 1), (0, -1)]),
        others([(8, 0), (-8, 0), (0, 2), (0, -2)]),
        others([(1, 0), (-1, 0)]),
    ]
    barrier = pltpu.get_barrier_semaphore()
    signal(barrier, near)

    def spread(k):
        if k > 0 and rounds[k - 1]:
            pl.semaphore_wait(round_sem.at[k - 1], len(rounds[k - 1]))
        if k < len(rounds):
            signal(round_sem.at[k], rounds[k])

    def send(src, dst, ss, rs, to):
        pltpu.make_async_remote_copy(
            src_ref=src, dst_ref=dst, send_sem=ss, recv_sem=rs, device_id=to, device_id_type=MESH
        ).start()

    def wait_for(ref, sem):
        pltpu.make_async_copy(ref, ref, sem).wait()

    def span(c):
        return pl.ds(starts[c], sizes[c])

    def send_prices(y, yb, ss, rs, c):
        at = span(c)
        send(y.at[0:2, at], yb.at[3:5, at], ss, rs.at[c], there(-1, -1))
        send(y.at[0:1, at], yb.at[5:6, at], ss, rs.at[c], there(-1, 0))
        send(y.at[1:4, at], yb.at[0:3, at], ss, rs.at[c], there(0, -1))

    def send_arrivals(fs, fv, fb, ss, rs, c):
        at = span(c)
        send(fs.at[3:5, at], fb.at[3:5, at], ss, rs.at[c], there(1, 1))
        send(fv, fb.at[5:6, at], ss, rs.at[c], there(1, 0))
        send(fs.at[0:3, at], fb.at[0:3, at], ss, rs.at[c], there(0, 1))

    def mix(values, weight):
        hi = values.astype(BF16)
        lo = (values - hi.astype(F32)).astype(BF16)
        both = jnp.dot(jnp.concatenate([hi, lo], axis=1), weight[...], preferred_element_type=F32)
        return both[:, :PANEL] + both[:, PANEL:]

    def pulled_gradients(y, yb, c):
        pulled = mix(yb[0:5, span(c), :].reshape(5 * sizes[c], PANEL), w_adj)
        pulled = pulled.reshape(5, sizes[c], PANEL)
        pulled = [pulled[k] for k in range(5)]
        pulled[3] = jnp.where(last, 0.0, pulled[3])
        pulled[4] = jnp.where(last, 0.0, pulled[4])
        short = lead[span(c), :] == 1
        rows = [y[t, span(c), :] for t in range(ROWS)]
        after = rows[1:] + [jnp.where(last, 0.0, yb[5, span(c), :])]
        grad_v = [rows[t] - after[t] for t in range(ROWS)]
        grad_s = [rows[t] - jnp.where(short, pulled[t], pulled[t + 1]) for t in range(ROWS)]
        return grad_v, grad_s

    def mix_arrivals(rows, fs, c):
        short = lead[span(c), :] == 1
        lagged = jnp.concatenate(
            [
                jnp.where(short, rows[0], 0.0),
                jnp.where(short, rows[1], rows[0]),
                jnp.where(short, rows[2], rows[1]),
                jnp.where(short, rows[3], rows[2]),
                jnp.where(short, 0.0, rows[3]),
            ],
            axis=0,
        )
        fs[:, span(c), :] = mix(lagged, w_fwd).reshape(5, sizes[c], PANEL)

    def arrivals(fb, c):
        early = [jnp.where(first, 0.0, fb[3 + k, span(c), :]) for k in range(2)]
        own = [fb[k, span(c), :] for k in range(3)]
        return early, [early[0], own[0] + early[1], own[1], own[2]]

    def balance_of(v_rows, s_rows, fb, receipts, c):
        before = [jnp.where(first, 0.0, fb[5, span(c), :])] + v_rows[:-1]
        return [v_rows[t] - before[t] + s_rows[t] - receipts[t] for t in range(ROWS)]

    def fold(values):
        return jnp.sum(values.reshape(values.shape[0] // 8, 8, PANEL), axis=0)

    loads[1].wait()
    for weight, dest in ((mixw[...], w_fwd), (mixw[...].T, w_adj)):
        hi = weight.astype(BF16)
        lo = (weight - hi.astype(F32)).astype(BF16)
        half = jnp.concatenate([hi, lo], axis=1)
        dest[...] = jnp.concatenate([half, half], axis=0)
    for cp in loads[2:5]:
        cp.wait()

    def send_start(c):
        send_arrivals(fs_1, v0.at[3:4, span(c)], fb_1, send_sem.at[0], f1_rs, c)

    for c in range(CHUNKS):
        mix_arrivals([s0[t, span(c), :] for t in range(ROWS)], fs_1, c)

    loads[0].wait()
    pl.semaphore_wait(barrier, len(near))
    for c in range(CHUNKS):
        send_prices(y0, yb0, send_sem.at[1], y0_rs, c)
    spread(0)

    for c in range(CHUNKS // 2):
        send_start(c)
    for cp in loads[5:]:
        cp.wait()

    primal = jnp.zeros((8, PANEL), F32)
    dual = jnp.zeros((8, PANEL), F32)

    def first_primal(c, primal):
        wait_for(yb0.at[:, span(c)], y0_rs.at[c])
        grad_v, grad_s = pulled_gradients(y0, yb0, c)
        ahead = []
        for t in range(ROWS):
            old_v = v0[t, span(c), :]
            new_v = jnp.maximum(old_v - STEP_ETA * (ch[t, span(c), :] - grad_v[t]), 0.0)
            v1[t, span(c), :] = new_v
            if t == ROWS - 1:
                fv_t[0, span(c), :] = 2.0 * new_v - old_v
            old_s = s0[t, span(c), :]
            top = cap[t, span(c), :].astype(F32)
            new_s = jnp.minimum(
                jnp.maximum(old_s - STEP_ETA * (cs[t, span(c), :] - grad_s[t]), 0.0), top
            )
            s1[t, span(c), :] = new_s
            primal = primal + fold((new_v - old_v) ** 2) + fold((new_s - old_s) ** 2)
            ahead.append(2.0 * new_s - old_s)
        mix_arrivals(ahead, fs_t, c)
        send_arrivals(fs_t, fv_t.at[:, span(c)], fb_t, send_sem.at[2], ft_rs, c)
        return primal

    def first_dual(c, dual):
        wait_for(fb_t.at[:, span(c)], ft_rs.at[c])
        _, receipts = arrivals(fb_t, c)
        v_rows = [2.0 * v1[t, span(c), :] - v0[t, span(c), :] for t in range(ROWS)]
        s_rows = [2.0 * s1[t, span(c), :] - s0[t, span(c), :] for t in range(ROWS)]
        ahead = balance_of(v_rows, s_rows, fb_t, receipts, c)
        for t in range(ROWS):
            bal1[t, span(c), :] = ahead[t]
            moved = STEP_ETA * (dem[t, span(c), :] - ahead[t])
            new_y = y0[t, span(c), :] + moved
            y1[t, span(c), :] = new_y
            dual = dual + fold((new_y - y0[t, span(c), :]) ** 2)
        if c < CHUNKS - 1:
            send_prices(y1, yb1, send_sem.at[3], y1_rs, c)
        return dual

    for c in range(CHUNKS + LAG):
        if c < CHUNKS:
            primal = first_primal(c, primal)
        if c == CHUNKS - 1:
            for k in range(CHUNKS // 2, CHUNKS):
                send_start(k)
        if c >= LAG:
            dual = first_dual(c - LAG, dual)
        if 0 < c <= len(rounds):
            spread(c)

    lane = lax.broadcasted_iota(jnp.int32, (1, PANEL), 1)
    primal = jnp.sum(primal, axis=0, keepdims=True)
    dual = jnp.sum(dual, axis=0, keepdims=True)
    half = PANEL // 2
    mine = jnp.where(
        lane < half, primal + pltpu.roll(primal, half, 1), dual + pltpu.roll(dual, half, 1)
    )
    row1[...] = mine
    for d in w_off:
        send(row1, rows1.at[w], wide_sem.at[0], wide_sem.at[1], there(d, 0))
    rows1[w] = mine
    send_prices(y1, yb1, send_sem.at[3], y1_rs, CHUNKS - 1)

    wait_for(rows1.at[0 : weeks - 1], wide_sem.at[1])
    mine = jnp.sum(rows1[...], axis=0)
    row2[...] = mine
    for d in range(1, regions):
        send(row2, rows2.at[r], wide_sem.at[2], wide_sem.at[3], there(0, d))
    rows2[r] = mine

    for c in range(CHUNKS):
        wait_for(yb1.at[:, span(c)], y1_rs.at[c])
        grad_v, grad_s = pulled_gradients(y1, yb1, c)
        for t in range(ROWS):
            ch[t, span(c), :] = ch[t, span(c), :] - grad_v[t]
            cs[t, span(c), :] = cs[t, span(c), :] - grad_s[t]

    s_sum[...] = dem[0] + dem[1] + dem[2] + dem[3]

    wait_for(rows2.at[0 : regions - 1], wide_sem.at[3])
    total = jnp.sum(rows2[...], axis=0)
    moved_primal = jnp.sum(jnp.where(lane < half, total, 0.0), axis=1, keepdims=True)
    moved_dual = jnp.sum(jnp.where(lane < half, 0.0, total), axis=1, keepdims=True)
    ratio = jnp.broadcast_to((moved_dual + EPS_MOVE) / (moved_primal + EPS_MOVE), (1, PANEL))
    weight = jnp.sqrt(jnp.sqrt(ratio))
    primal_step = STEP_ETA / weight
    dual_step = STEP_ETA * weight

    owners = weeks // 4
    quarter = panels // 4

    def quarter_at(k):
        q = lax.rem(lax.div(w, owners) + k, 4)
        return q, pl.ds(pl.multiple_of(q * quarter, 8), quarter)

    for k in QUARTERS:
        _, at = quarter_at(k)
        sums = jnp.zeros((quarter, PANEL), F32)
        for t in range(ROWS):
            new_s = jnp.minimum(
                jnp.maximum(s1[t, at, :] - primal_step * cs[t, at, :], 0.0), cap[t, at, :].astype(F32)
            )
            s2[t, at, :] = new_s
            sums = sums + new_s
        s_sum[at, :] = s_sum[at, :] + sums
        m_send[at, :] = mix(sums, w_fwd)
        send(m_send.at[at], m_recv.at[at], wide_sem.at[4], m_rs.at[k], there(0, 1))

    def last_arrivals(c):
        for t in range(ROWS):
            v2[t, span(c), :] = jnp.maximum(v1[t, span(c), :] - primal_step * ch[t, span(c), :], 0.0)
        mix_arrivals([s2[t, span(c), :] for t in range(ROWS)], fs_2, c)
        send_arrivals(fs_2, v2.at[3:4, span(c)], fb_2, send_sem.at[4], f2_rs, c)

    for c in range(EARLY):
        last_arrivals(c)

    for k in QUARTERS:
        q, at = quarter_at(k)
        wait_for(m_recv.at[at], m_rs.at[k])
        net[at, :] = m_recv[at, :] - s_sum[at, :]
        for j in range(0 if k else 1, owners):
            to = q * owners + lax.rem(w + j, owners)
            send(net.at[pl.ds(to * piece, piece)], a1.at[w], wide_sem.at[5], wide_sem.at[6], (to, r))
    a1[w] = net[pl.ds(w * piece, piece), :]

    for c in range(EARLY, CHUNKS - LATE):
        last_arrivals(c)

    for c in range(CHUNKS):
        wait_for(fb_1.at[:, span(c)], f1_rs.at[c])
        _, receipts = arrivals(fb_1, c)
        v_rows = [v0[t, span(c), :] for t in range(ROWS)]
        s_rows = [s0[t, span(c), :] for t in range(ROWS)]
        rows = balance_of(v_rows, s_rows, fb_1, receipts, c)
        for t in range(ROWS):
            bal1[t, span(c), :] = 0.5 * (bal1[t, span(c), :] + rows[t])

    wait_for(a1.at[0 : weeks - 1], wide_sem.at[6])
    running = jnp.zeros((piece, PANEL), F32)
    for k in range(weeks):
        a2[k] = running
        running = running + a1[k]
    for d in w_off:
        to = there(d, 0)
        send(a2.at[to[0]], pref.at[pl.ds(w * piece, piece)], wide_sem.at[7], wide_sem.at[8], to)
    pref[pl.ds(w * piece, piece), :] = a2[w]

    for c in range(CHUNKS - LATE, CHUNKS):
        last_arrivals(c)

    for c in range(CHUNKS):
        wait_for(fb_2.at[:, span(c)], f2_rs.at[c])
        early, receipts = arrivals(fb_2, c)
        v_rows = [v2[t, span(c), :] for t in range(ROWS)]
        s_rows = [s2[t, span(c), :] for t in range(ROWS)]
        rows = balance_of(v_rows, s_rows, fb_2, receipts, c)
        flow = -early[0] - early[1]
        for t in range(ROWS):
            wanted = dem[t, span(c), :]
            y2[t, span(c), :] = y1[t, span(c), :] + dual_step * (
                wanted - 2.0 * rows[t] + bal1[t, span(c), :]
            )
            flow = flow + (receipts[t] - s_rows[t] - wanted)
            pj[t, span(c), :] = flow
    for k, landing in enumerate((fb_1, yb0, fb_t, yb1, fb_2)):
        wait_for(landing, send_sem.at[k])
    wait_for(rows1.at[0 : weeks - 1], wide_sem.at[0])
    wait_for(rows2.at[0 : regions - 1], wide_sem.at[2])
    wait_for(m_recv, wide_sem.at[4])
    wait_for(a1.at[0 : weeks - 1], wide_sem.at[5])
    wait_for(a2.at[0 : weeks - 1], wide_sem.at[7])
    wait_for(pref.at[0 : panels - piece], wide_sem.at[8])


def finish(v2, s2, y2, pj, pref, stock_out, ship_out, dual_out, proj_out, total, sem):
    copies = []
    for k, (src, dst) in enumerate(((v2, stock_out), (s2, ship_out), (y2, dual_out))):
        copies.append(pltpu.make_async_copy(src, dst, sem.at[k]))
        copies[-1].start()
    for t in range(ROWS):
        total[t] = pj[t] + pref[...]
        copies.append(pltpu.make_async_copy(total.at[t], proj_out.at[t], sem.at[3 + t]))
        copies[-1].start()
    for cp in copies:
        cp.wait()


def shards(weeks, regions, stock, ship, dual, demand, hold, cost, cap, lead, mix):
    items = stock.shape[-1]
    panels = items // PANEL

    def in_hbm(a, *shape):
        return pltpu.with_memory_space_constraint(a.reshape(shape), pltpu.HBM)

    def view(a):
        return in_hbm(a, ROWS, panels, PANEL)

    slab = (ROWS, panels, PANEL)

    def vmem(*shape, dtype=F32):
        return pltpu.VMEM(shape, dtype)

    def sems(n):
        return pltpu.SemaphoreType.DMA((n,))

    scratch = (
        [vmem(*slab)] * 6
        + [vmem(*slab, dtype=jnp.int32), vmem(panels, PANEL, dtype=jnp.int32), vmem(PANEL, PANEL)]
        + [vmem(2 * PANEL, 2 * PANEL, dtype=BF16)] * 2
        + [vmem(*slab)] * 4
        + [vmem(6, panels, PANEL)] * 2
        + [vmem(5, panels, PANEL), vmem(1, panels, PANEL), vmem(6, panels, PANEL)]
        + [vmem(5, panels, PANEL), vmem(6, panels, PANEL)] * 2
        + [vmem(panels, PANEL)] * 4
        + [vmem(weeks, panels // weeks, PANEL)] * 2
        + [vmem(1, PANEL), vmem(weeks, 1, PANEL), vmem(1, PANEL), vmem(regions, 1, PANEL)]
        + [sems(9), sems(5), sems(9), pltpu.SemaphoreType.REGULAR((3,))]
        + [sems(CHUNKS)] * 5
        + [sems(4)]
    )
    parts = pl.pallas_call(
        functools.partial(kernel, weeks, regions, panels),
        out_shape=[jax.ShapeDtypeStruct(slab, F32)] * 4
        + [jax.ShapeDtypeStruct((panels, PANEL), F32)],
        in_specs=[pl.BlockSpec(memory_space=pltpu.HBM)] * 9,
        out_specs=[pl.BlockSpec(memory_space=pltpu.VMEM)] * 5,
        scratch_shapes=scratch,
        compiler_params=pltpu.CompilerParams(
            collective_id=0, has_side_effects=True, vmem_limit_bytes=40 * 1024 * 1024
        ),
        cost_estimate=pl.CostEstimate(
            flops=2 * 6 * 5 * 5 * panels * PANEL * PANEL,
            bytes_accessed=12 * 4 * ROWS * panels * PANEL,
            transcendentals=0,
        ),
        name="primal_dual",
    )(
        view(stock), view(ship), view(dual), view(demand), view(hold), view(cost), view(cap),
        in_hbm(lead, panels, PANEL), in_hbm(mix, PANEL, PANEL),
    )
    outs = pl.pallas_call(
        finish,
        out_shape=[jax.ShapeDtypeStruct(slab, F32)] * 4,
        in_specs=[pl.BlockSpec(memory_space=pltpu.VMEM)] * 5,
        out_specs=[pl.BlockSpec(memory_space=pltpu.HBM)] * 4,
        scratch_shapes=[vmem(*slab), pltpu.SemaphoreType.DMA((3 + ROWS,))],
        compiler_params=pltpu.CompilerParams(vmem_limit_bytes=8 * 1024 * 1024),
        name="finish",
    )(*parts)
    return tuple(o.reshape(ROWS, 1, items) for o in outs)


def solution(mesh):
    block = P("week", "region", None)
    in_specs = (block,) * 7 + (P("region", None), P("region", None, None))
    body = functools.partial(shards, mesh.shape["week"], mesh.shape["region"])
    return jax.shard_map(
        body, mesh=mesh, in_specs=in_specs, out_specs=(block,) * 4, check_vma=False
    )
```
